32 devices in a mesh: groups: 2 (over y), trades: 8 (over z, x), dates: 2 (over core).
Axes of the slice: x: 2, y: 2, z: 4, core: 2. Of those that a mesh axis runs over, the one named last changes fastest.
Arguments:
- basis_values: bfloat16 [8, 256, 256], P('dates', 'groups'), parts along dimension 1, may hold values from -6 to 6
- coefficients: bfloat16 [8192, 256], P('trades'), may hold values from -0.0625 to 0.0625
- set_map: int32 [8192], P('trades'), may hold values from 0 to 255, as said below
- trade_type: int32 [8192], P('trades'), may hold values from 0 to 15
- type_gain: float32 [8, 16], P('dates'), may hold values from 0.25 to 4
- set_lags: int32 [256], replicated, may hold values from 1 to 2
- thresholds: float32 [256], replicated, may hold values from -1 to 1
Outputs:
- coef_grad: float32 [16384, 256], P(('groups', 'trades'), 'dates'), parts along dimension 0
The draws below stay inside these ranges and needn't reach their ends.
There are 2 independent parts, one for each index of `groups`. The reference program is written for one: setup_inputs(seed, part) draws one part's arguments, and reference() takes and returns one part's arrays. A program takes and returns all parts, laid end to end along the dimension named above; an argument that names none is the same for every part. Nothing has to cross between parts.
Inputs may be any that keep to these rules, and one draw needn't show every extreme that they name: `set_map`: in every aligned block of 1024 trades, exactly 128 trades fall in each group of 32 consecutive netting sets (sets g * 32 to (g + 1) * 32 - 1).
All inputs are finite; a program needn't handle non-finite values.
Results may differ from the reference program's by a relative error of at most 0.0018.
Values may be sent and summed in bfloat16 or wider, within the bound.
No kernel may reach another device: no remote copies, remote signals or barrier semaphores. Data moves between devices by JAX's collectives and lax.ppermute only.
A program may use at most 64 MiB of HBM per device.

```python
import math
import jax
import jax.numpy as jnp
from jax import lax

K = 256
NSETS = 256
NTYPE = 16
LAG_MAX = 2
TR_DEV = 1024
TRADES = 8192
PATHS = 128
DATES = 8


def draw_set_map(key, part):
    block_count = TRADES // TR_DEV
    per_group = TR_DEV // block_count
    group_sets = NSETS // block_count
    first_key = jax.random.fold_in(key, 11)
    second_key = jax.random.fold_in(key, 23)
    groups_base = jnp.tile(jnp.arange(block_count, dtype=jnp.int32), per_group)
    block_keys = jax.random.split(first_key, block_count)
    shuffled = jax.vmap(lambda one_key: jax.random.permutation(one_key, groups_base))(block_keys)
    within = jax.random.randint(second_key, (TRADES,), 0, group_sets, dtype=jnp.int32)
    return (shuffled.reshape(TRADES) * group_sets + within).astype(jnp.int32)


def place_ends(drawn, rng, least, high):
    index_at = [jax.random.randint(jax.random.fold_in(rng, axis), (), 0, length) for axis, length in enumerate(drawn.shape)]
    longest = drawn.shape.index(max(drawn.shape))
    next_to = index_at[:longest] + [(index_at[longest] + 1) % drawn.shape[longest]] + index_at[longest + 1:]
    return drawn.at[tuple(index_at)].set(least).at[tuple(next_to)].set(high)


def levels(rng, extent, cuts, low, high):
    factor_of, own = 1.0, jax.random.fold_in(rng, 6)
    for axis_at, blocks in cuts:
        steps = jnp.exp(jax.random.uniform(jax.random.fold_in(own, axis_at), (blocks,), jnp.float32, low / len(cuts), high / len(cuts)))
        factor_of = factor_of * jnp.repeat(steps, extent[axis_at] // blocks).reshape([-1 if axis == axis_at else 1 for axis in range(len(extent))])
    return factor_of


def normal_values(stream_key, shape, deviation, most, cuts=(), kind=jnp.bfloat16):
    result = jax.random.normal(stream_key, shape, jnp.float32) * deviation
    if len(cuts) > 0:
        result = levels(stream_key, shape, cuts, -0.22, 0.18) * result
    return jnp.clip(result, min=-most, max=most).astype(kind)


def setup_inputs(seed: int = 0, part: int = 0) -> dict:
    key_of = jax.random.split(jax.random.key(seed), 8)
    own_keys = jax.random.split(jax.random.fold_in(key_of[7], part), 8)
    return {
        "basis_values": normal_values(own_keys[0], (DATES, PATHS, K), 1.0, 6.0, ((0, 2),)),
        "coefficients": normal_values(key_of[1], (TRADES, K), (K * TRADES // NSETS) ** -0.5, 0.0625, ((0, 8),)),
        "set_map": draw_set_map(jax.random.fold_in(key_of[7], 71), part),
        "trade_type": place_ends(jax.random.randint(key_of[3], (TRADES,), 0, NTYPE), jax.random.fold_in(key_of[3], 1), 0, NTYPE - 1).astype(jnp.int32),
        "type_gain": jnp.clip(jnp.exp(math.log(4.0) - 2.7725887 * jax.random.uniform(key_of[4], (DATES, NTYPE), jnp.float32) ** levels(key_of[4], (DATES, NTYPE), ((0, 2),), -0.2, 0.2)), 0.25, 4.0),
        "set_lags": place_ends(jax.random.randint(key_of[5], (NSETS,), 1, LAG_MAX + 1), jax.random.fold_in(key_of[5], 1), 1, LAG_MAX).astype(jnp.int32),
        "thresholds": jnp.clip(jax.random.uniform(key_of[6], (NSETS,), jnp.float32, -1.0, 1.0), -1.0, 1.0),
    }


def reference(basis_values, coefficients, set_map, trade_type, type_gain, set_lags, thresholds):
    trade_count = coefficients.shape[0]
    block_count = trade_count // TR_DEV
    date_count = basis_values.shape[0]
    path_count = basis_values.shape[1]
    set_ids = jnp.arange(NSETS, dtype=jnp.int32)
    basis_wide = basis_values.astype(jnp.float32)

    def block_inputs(block_index):
        first_row = (block_index * TR_DEV).astype(jnp.int32)
        coef_block = lax.dynamic_slice_in_dim(coefficients, first_row, TR_DEV, 0).astype(jnp.float32)
        set_block = lax.dynamic_slice_in_dim(set_map, first_row, TR_DEV, 0)
        type_block = lax.dynamic_slice_in_dim(trade_type, first_row, TR_DEV, 0)
        trade_gain = jnp.take(type_gain, type_block, axis=1)
        return (coef_block, set_block, trade_gain)

    def add_block(block_index, netted):
        coef_block, set_block, trade_gain = block_inputs(block_index)
        raw_value = jnp.einsum('dpk,tk->dpt', basis_wide, coef_block)
        prices = (raw_value * trade_gain[:, None, :]).astype(jnp.bfloat16)
        prices = lax.optimization_barrier(prices)
        membership = (set_block[:, None] == set_ids[None, :]).astype(jnp.float32)
        return netted + jnp.einsum('dpt,ts->pds', prices.astype(jnp.float32), membership)
    netted = lax.fori_loop(0, block_count, add_block, jnp.zeros((path_count, date_count, NSETS), jnp.float32))
    padded = jnp.pad(netted, ((0, 0), (LAG_MAX, 0), (0, 0)))
    padded_back_zeros = jnp.zeros((path_count, LAG_MAX, NSETS), jnp.float32)
    collateral = jnp.zeros_like(netted)
    for lag_value in range(1, LAG_MAX + 1):
        lag_mask = (set_lags == lag_value).astype(jnp.float32)
        collateral = collateral + lag_mask * padded[:, LAG_MAX - lag_value:LAG_MAX - lag_value + date_count, :]
    exposure = jnp.maximum(netted - collateral - thresholds, 0.0)
    direct_term = exposure * (2.0 / math.sqrt(date_count * path_count))
    padded_back = jnp.concatenate([direct_term, padded_back_zeros], axis=1)
    adjoint = direct_term
    for lag_value in range(1, LAG_MAX + 1):
        lag_mask = (set_lags == lag_value).astype(jnp.float32)
        adjoint = adjoint - lag_mask * padded_back[:, lag_value:lag_value + date_count, :]
    adjoint = lax.optimization_barrier(adjoint.astype(jnp.bfloat16))
    adjoint_wide = adjoint.astype(jnp.float32)

    def grad_block(block_index):
        coef_block, set_block, trade_gain = block_inputs(block_index)
        spread = jnp.take(adjoint_wide, set_block, axis=2)
        scaled = (jnp.transpose(spread, (1, 0, 2)) * trade_gain[:, None, :]).astype(jnp.bfloat16)
        scaled = lax.optimization_barrier(scaled)
        return jnp.einsum('dpt,dpk->tk', scaled.astype(jnp.float32), basis_wide)
    grads = lax.map(grad_block, jnp.arange(block_count, dtype=jnp.int32))
    return grads.reshape(trade_count, K)
```

```python
import math

import jax
import jax.numpy as jnp
from jax import lax
from jax.sharding import PartitionSpec as P

LAG_MAX = 2


def swap_sum(blocks_of, axis):
    peers = lax.axis_size(axis)
    me = lax.axis_index(axis)
    arrived = []
    for step in range(1, peers):
        pairs = [(i, (i + step) % peers) for i in range(peers)]
        arrived.append(lax.ppermute(blocks_of((me + step) % peers), axis, pairs))
    total = blocks_of(me)
    for part in arrived:
        total = total + part
    return total


def on_device(basis_values, coefficients, set_map, trade_type, type_gain, set_lags, thresholds):
    local_dates, path_count, depth = basis_values.shape
    trade_local = coefficients.shape[0]
    set_count = thresholds.shape[0]
    type_count = type_gain.shape[1]
    trade_peers = lax.axis_size("trades")
    date_peers = lax.axis_size("dates")
    blocks = trade_peers * date_peers
    block_paths = path_count // blocks
    dates = local_dates * date_peers
    rows = local_dates * path_count
    loss_scale = 2.0 / math.sqrt(dates * path_count)
    member = (set_map[:, None] == jnp.arange(set_count, dtype=jnp.int32)[None, :]).astype(jnp.bfloat16)
    type_onehot = (trade_type[:, None] == jnp.arange(type_count, dtype=jnp.int32)[None, :]).astype(
        jnp.float32
    )
    own_gain = jnp.einsum(
        "dy,ty->dt",
        type_gain,
        type_onehot,
        precision=lax.Precision.HIGHEST,
        preferred_element_type=jnp.float32,
    )
    basis_rows = basis_values.reshape(rows, depth)
    raw_value = jnp.einsum("rk,tk->rt", basis_rows, coefficients, preferred_element_type=jnp.float32)
    prices = raw_value.reshape(local_dates, path_count, trade_local) * own_gain[:, None, :]
    prices = prices.astype(jnp.bfloat16).reshape(rows, trade_local)
    partial = jnp.dot(prices, member, preferred_element_type=jnp.float32)
    partial = partial.reshape(local_dates, blocks, block_paths, set_count).transpose(1, 0, 2, 3)
    partial = partial.astype(jnp.float16)
    arrived = lax.all_to_all(partial, ("trades", "dates"), split_axis=0, concat_axis=0, tiled=True)
    arrived = arrived.reshape(trade_peers, dates, block_paths, set_count)
    netted = jnp.sum(arrived.astype(jnp.float32), axis=0)
    collateral = jnp.zeros_like(netted)
    padded = jnp.pad(netted, ((LAG_MAX, 0), (0, 0), (0, 0)))
    for lag_value in range(1, LAG_MAX + 1):
        lag_mask = (set_lags == lag_value).astype(jnp.float32)
        collateral = collateral + lag_mask * padded[LAG_MAX - lag_value : LAG_MAX - lag_value + dates]
    direct_term = jnp.maximum(netted - collateral - thresholds, 0.0) * loss_scale
    padded_back = jnp.pad(direct_term, ((0, LAG_MAX), (0, 0), (0, 0)))
    adjoint = direct_term
    for lag_value in range(1, LAG_MAX + 1):
        lag_mask = (set_lags == lag_value).astype(jnp.float32)
        adjoint = adjoint - lag_mask * padded_back[lag_value : lag_value + dates]
    adjoint = adjoint.astype(jnp.bfloat16).reshape(1, date_peers, local_dates, block_paths, set_count)
    adjoint = jnp.broadcast_to(adjoint, (trade_peers,) + adjoint.shape[1:])
    adjoint = adjoint.reshape(blocks, local_dates, block_paths, set_count)
    adjoint = lax.all_to_all(adjoint, ("trades", "dates"), split_axis=0, concat_axis=0, tiled=True)
    adjoint = adjoint.transpose(1, 0, 2, 3).reshape(rows, set_count)
    spread = jnp.einsum("ts,rs->tr", member, adjoint, preferred_element_type=jnp.float32)
    scaled = spread.reshape(trade_local, local_dates, path_count) * own_gain.T[:, :, None]
    scaled = scaled.astype(jnp.bfloat16).reshape(trade_local, rows)
    own_depth = depth // date_peers

    def part_of(which):
        columns = lax.dynamic_slice_in_dim(basis_rows, which * own_depth, own_depth, 1)
        return jnp.dot(scaled, columns, preferred_element_type=jnp.float32)

    return swap_sum(part_of, "dates")


def solution(mesh):
    return jax.shard_map(
        on_device,
        mesh=mesh,
        in_specs=(
            P("dates", "groups", None),
            P("trades", None),
            P("trades"),
            P("trades"),
            P("dates", None),
            P(),
            P(),
        ),
        out_specs=P(("groups", "trades"), "dates"),
        check_vma=False,
    )
```

```python
import functools
import math

import jax
import jax.numpy as jnp
from jax import lax
from jax.experimental import pallas as pl
from jax.experimental.pallas import tpu as pltpu
from jax.sharding import PartitionSpec as P

LAG_MAX = 2
NT = (((1,), (1,)), ((), ()))
VMEM_BYTES = 40 * 1024 * 1024


def in_hbm(*arrays):
    return [pltpu.with_memory_space_constraint(array, pltpu.HBM) for array in arrays]


def whole(*shape):
    return pl.BlockSpec(shape, lambda *_: (0,) * len(shape))


def netting_kernel(
    basis_ref, coef_ref, set_ref, type_ref, gain_ref, lags_ref, limits_ref, out_ref, lags_out_ref, limits_out_ref
):
    lags_out_ref[...] = lags_ref[...]
    limits_out_ref[...] = limits_ref[...]
    dates, paths, depth = basis_ref.shape
    blocks, _, block_paths, set_count = out_ref.shape
    trades = coef_ref.shape[0]
    gain = jnp.zeros((dates, trades), jnp.float32)
    for which in range(gain_ref.shape[1]):
        gain = jnp.where(type_ref[...] == which, gain_ref[:, which : which + 1], gain)
    member = lax.broadcasted_iota(jnp.int32, (set_count, trades), 0) == set_ref[...]
    member = member.astype(jnp.float32).astype(jnp.bfloat16)
    rows = basis_ref[...].reshape(dates * paths, depth)
    raw = lax.dot_general(rows, coef_ref[...], NT, preferred_element_type=jnp.float32)
    prices = raw.reshape(dates, paths, trades) * gain[:, None, :]
    prices = prices.astype(jnp.bfloat16).reshape(dates * paths, trades)
    netted = lax.dot_general(prices, member, NT, preferred_element_type=jnp.float32)
    netted = netted.reshape(dates, blocks, block_paths, set_count)
    for date in range(dates):
        out_ref[:, date] = netted[date]


def net_own(basis_values, coefficients, set_map, trade_type, type_gain, set_lags, thresholds, blocks):
    set_count = thresholds.shape[0]
    dates, paths, depth = basis_values.shape
    trades = coefficients.shape[0]
    block_paths = paths // blocks
    span = math.gcd(paths, max(block_paths, 128))
    shape = (blocks, dates, block_paths, set_count)
    return pl.pallas_call(
        netting_kernel,
        grid=(paths // span,),
        in_specs=[
            pl.BlockSpec((dates, span, depth), lambda i: (0, i, 0)),
            whole(trades, depth),
            whole(1, trades),
            whole(1, trades),
            whole(dates, type_gain.shape[1]),
            whole(1, set_count),
            whole(1, set_count),
        ],
        out_specs=[
            pl.BlockSpec((span // block_paths,) + shape[1:], lambda i: (i, 0, 0, 0)),
            whole(1, set_count),
            whole(1, set_count),
        ],
        out_shape=[
            pltpu.VMEM(shape, jnp.float32),
            pltpu.VMEM((1, set_count), jnp.int32),
            pltpu.VMEM((1, set_count), jnp.float32),
        ],
        compiler_params=pltpu.CompilerParams(vmem_limit_bytes=VMEM_BYTES),
    )(
        *in_hbm(
            basis_values,
            coefficients,
            set_map.reshape(1, trades),
            trade_type.reshape(1, trades),
            type_gain,
            set_lags.reshape(1, set_count),
            thresholds.reshape(1, set_count),
        )
    )


def adjoint_kernel(scale, netted_ref, lags_ref, limits_ref, out_ref):
    dates, block_paths, set_count = netted_ref.shape
    lag = lags_ref[...].reshape(1, set_count)
    limit = limits_ref[...].reshape(1, set_count)
    masks = [(lag == value).astype(jnp.float32) for value in range(1, LAG_MAX + 1)]
    netted = [netted_ref[date] for date in range(dates)]
    direct = []
    for date in range(dates):
        collateral = jnp.zeros_like(netted[date])
        for value, mask in enumerate(masks, 1):
            if date >= value:
                collateral = collateral + mask * netted[date - value]
        direct.append(jnp.maximum(netted[date] - collateral - limit, 0.0) * scale)
    adjoints = []
    for date in range(dates):
        adjoint = direct[date]
        for value, mask in enumerate(masks, 1):
            if date + value < dates:
                adjoint = adjoint - mask * direct[date + value]
        adjoints.append(adjoint)
    block = jnp.concatenate(adjoints, axis=0).astype(jnp.bfloat16)
    for peer in range(out_ref.shape[0]):
        out_ref[peer] = block


def adjoint_of(netted, set_lags, thresholds, scale, peers):
    dates, block_paths, set_count = netted.shape
    return pl.pallas_call(
        functools.partial(adjoint_kernel, scale),
        out_shape=pltpu.VMEM((peers, dates * block_paths, set_count), jnp.bfloat16),
        compiler_params=pltpu.CompilerParams(vmem_limit_bytes=VMEM_BYTES),
    )(netted, set_lags, thresholds)


def grad_kernel(carry, *refs):
    if carry:
        total_ref, member_ref, gain_ref, adjoint_ref, basis_ref, out_ref = refs
    else:
        member_ref, gain_ref, adjoint_ref, basis_ref, out_ref = refs
    rows = adjoint_ref.shape[0]
    period = gain_ref.shape[1]
    spread = lax.dot_general(member_ref[...], adjoint_ref[...], NT, preferred_element_type=jnp.float32)
    gain = gain_ref[...]
    scaled = [
        (spread[:, first : first + period] * gain).astype(jnp.bfloat16) for first in range(0, rows, period)
    ]
    scaled = jnp.concatenate(scaled, axis=1)
    part = jnp.dot(scaled, basis_ref[...], preferred_element_type=jnp.float32)
    last = pl.program_id(1)

    if carry:
        part = jnp.where(last == 0, total_ref[...], 0.0) + part

    @pl.when(last == 0)
    def _():
        out_ref[...] = part

    @pl.when(last > 0)
    def _():
        out_ref[...] += part


def add_grad(total, member, gain, adjoint, basis, final):
    trades, set_count = member.shape
    rows, depth = basis.shape
    period = gain.shape[1]
    span = math.gcd(rows, max(period, 512))
    tile = math.gcd(trades, 1024)
    shape = (trades, depth)
    carry = total is not None
    row = lambda i, j: (i, 0)
    return pl.pallas_call(
        functools.partial(grad_kernel, carry),
        grid=(trades // tile, rows // span),
        in_specs=([pl.BlockSpec((tile, depth), row)] if carry else [])
        + [
            pl.BlockSpec((tile, set_count), row),
            pl.BlockSpec((tile, period), row),
            pl.BlockSpec((span, set_count), lambda i, j: (j, 0)),
            pl.BlockSpec((span, depth), lambda i, j: (j, 0)),
        ],
        out_specs=pl.BlockSpec((tile, depth), row),
        out_shape=jax.ShapeDtypeStruct(shape, jnp.float32) if final else pltpu.VMEM(shape, jnp.float32),
        compiler_params=pltpu.CompilerParams(vmem_limit_bytes=VMEM_BYTES),
        cost_estimate=pl.CostEstimate(
            flops=2 * trades * rows * (set_count + depth), bytes_accessed=4 * trades * depth, transcendentals=0
        ),
    )(*([total] if carry else []), member, gain, adjoint, basis)


def from_dates(pieces_of, like):
    peers = lax.axis_size("dates")
    me = lax.axis_index("dates")
    size = like.shape[0]
    full = jnp.zeros((size * peers,) + like.shape[1:], like.dtype)
    for step in range(peers):
        piece = pieces_of((me + step) % peers)
        if step:
            piece = lax.ppermute(piece, "dates", [(i, (i + step) % peers) for i in range(peers)])
        owner = (me - step) % peers
        full = lax.dynamic_update_slice_in_dim(full, piece, owner * size, 0)
    return full


def on_device(basis_values, coefficients, set_map, trade_type, type_gain, set_lags, thresholds):
    local_dates, path_count, depth = basis_values.shape
    trade_local = coefficients.shape[0]
    set_count = thresholds.shape[0]
    type_count = type_gain.shape[1]
    trade_peers = lax.axis_size("trades")
    date_peers = lax.axis_size("dates")
    me = lax.axis_index("dates")
    blocks = trade_peers * date_peers
    block_paths = path_count // blocks
    dates = local_dates * date_peers
    own_depth = depth // date_peers
    loss_scale = 2.0 / math.sqrt(dates * path_count)
    partial, lags, limits = net_own(
        basis_values, coefficients, set_map, trade_type, type_gain, set_lags, thresholds, blocks
    )
    partial = partial.astype(jnp.float16)
    arrived = lax.all_to_all(partial, ("trades", "dates"), split_axis=0, concat_axis=0, tiled=True)
    netted = jnp.sum(
        arrived.reshape(trade_peers, dates, block_paths, set_count).astype(jnp.float32), axis=0
    )
    adjoint = adjoint_of(netted, lags, limits, loss_scale, trade_peers)
    basis_late, gain_late, set_late, type_late, adjoint = lax.optimization_barrier(
        (basis_values, type_gain, set_map, trade_type, adjoint)
    )
    adjoint = lax.all_to_all(adjoint, "trades", split_axis=0, concat_axis=0, tiled=True)
    adjoint = adjoint.reshape(trade_peers * dates * block_paths, set_count)

    def own_columns(which):
        return lax.dynamic_slice_in_dim(basis_late, which * own_depth, own_depth, 2)

    basis = from_dates(own_columns, basis_late[:, :, :own_depth])
    basis = basis.reshape(dates, trade_peers, date_peers, block_paths, own_depth).transpose(2, 1, 0, 3, 4)
    basis = basis.reshape(date_peers, trade_peers * dates * block_paths, own_depth)
    gain = from_dates(lambda which: gain_late, gain_late)
    period = dates * block_paths
    while period % 128:
        period *= 2
    gain_rows = jnp.tile(jnp.repeat(gain, block_paths, axis=0), (period // (dates * block_paths), 1))
    member = (set_late[:, None] == jnp.arange(set_count, dtype=jnp.int32)[None, :]).astype(jnp.bfloat16)
    trade_gain = jnp.zeros((trade_local, period), jnp.float32)
    for which in range(type_count):
        trade_gain = jnp.where(type_late[:, None] == which, gain_rows[:, which][None, :], trade_gain)
    total = None
    for step in range(date_peers):
        there = adjoint
        if step:
            there = lax.ppermute(adjoint, "dates", [(i, (i + step) % date_peers) for i in range(date_peers)])
        rows = lax.dynamic_index_in_dim(basis, (me - step) % date_peers, 0, keepdims=False)
        total = add_grad(total, member, trade_gain, there, rows, step == date_peers - 1)
    return total


def solution(mesh):
    return jax.shard_map(
        on_device,
        mesh=mesh,
        in_specs=(
            P("dates", "groups", None),
            P("trades", None),
            P("trades"),
            P("trades"),
            P("dates", None),
            P(),
            P(),
        ),
        out_specs=P(("groups", "trades"), "dates"),
        check_vma=False,
    )
```

```python
import functools
import math

import jax
import jax.numpy as jnp
from jax import lax
from jax.experimental import pallas as pl
from jax.experimental.pallas import tpu as pltpu
from jax.sharding import PartitionSpec as P

LAG_MAX = 2
SPAN = 64
NT = (((1,), (1,)), ((), ()))
TN = (((0,), (0,)), ((), ()))
TT = (((0,), (1,)), ((), ()))
PARAMS = pltpu.CompilerParams(vmem_limit_bytes=40 * 1024 * 1024)
SCALAR = pl.BlockSpec(memory_space=pltpu.SMEM)
LOCAL = pl.BlockSpec(memory_space=pltpu.VMEM)


def in_hbm(*arrays):
    return [pltpu.with_memory_space_constraint(array, pltpu.HBM) for array in arrays]


def kept(array):
    return pltpu.VMEM(array.shape, array.dtype)


def shifted(array, axis, step):
    peers = lax.axis_size(axis)
    return lax.ppermute(array, axis, [(i, (i + step) % peers) for i in range(peers)])


def gain_of_trades(gain, types):
    rows = jnp.zeros((gain.shape[0], types.shape[1]), jnp.float32)
    for which in range(gain.shape[1]):
        rows = jnp.where(types == which, gain[:, which : which + 1], rows)
    return rows


def net_paths(me, basis_ref, coef, gain, member, out_ref):
    dates, _, depth = basis_ref.shape
    peers, rows, set_count = out_ref.shape
    block_paths = rows // dates
    paths = peers * block_paths
    trades = coef.shape[0]
    span = math.gcd(paths, max(SPAN, block_paths))
    for first in range(0, paths, span):
        at = pl.multiple_of(me * paths + first, span)
        basis = basis_ref[:, pl.ds(at, span), :].reshape(dates * span, depth)
        raw = lax.dot_general(basis, coef, NT, preferred_element_type=jnp.float32)
        prices = raw.reshape(dates, span, trades) * gain[:, None, :]
        prices = prices.astype(jnp.bfloat16).reshape(dates * span, trades)
        netted = lax.dot_general(prices, member, NT, preferred_element_type=jnp.float32)
        netted = netted.reshape(dates, span // block_paths, block_paths, set_count)
        for date in range(dates):
            out_ref[
                pl.ds(first // block_paths, span // block_paths), pl.ds(date * block_paths, block_paths)
            ] = netted[date]


def first_net_kernel(
    me_ref, basis_ref, coef_ref, set_ref, type_ref, gain_ref, lags_ref, limits_ref, out_ref, member_ref, *copies
):
    set_count, trades = member_ref.shape
    member = lax.broadcasted_iota(jnp.int32, (set_count, trades), 0) == set_ref[...]
    member = member.astype(jnp.float32).astype(jnp.bfloat16)
    gain = gain_of_trades(gain_ref[...], type_ref[...])
    net_paths(me_ref[0], basis_ref, coef_ref[...], gain, member, out_ref)
    member_ref[...] = member
    for given, copy in zip((basis_ref, coef_ref, type_ref, gain_ref, lags_ref, limits_ref), copies, strict=True):
        copy[...] = given[...]


def next_net_kernel(me_ref, basis_ref, coef_ref, type_ref, gain_ref, member_ref, out_ref):
    gain = gain_of_trades(gain_ref[...], type_ref[...])
    net_paths(me_ref[0], basis_ref, coef_ref[...], gain, member_ref[...], out_ref)


def pricing_cost(basis, coef, set_count, owners):
    dates, paths, depth = basis.shape
    return pl.CostEstimate(
        flops=2 * dates * paths // owners * coef.shape[0] * (depth + set_count),
        bytes_accessed=coef.size * 2,
        transcendentals=0,
    )


def net_first(me, basis, coef, sets, types, gain, lags, limits, peers, owners):
    dates, paths, _ = basis.shape
    set_count = limits.shape[1]
    block_paths = paths // (peers * owners)
    return pl.pallas_call(
        first_net_kernel,
        in_specs=[SCALAR] + [LOCAL] * 7,
        out_specs=[LOCAL] * 8,
        out_shape=[
            pltpu.VMEM((peers, dates * block_paths, set_count), jnp.float32),
            pltpu.VMEM((set_count, coef.shape[0]), jnp.bfloat16),
        ]
        + [kept(array) for array in (basis, coef, types, gain, lags, limits)],
        compiler_params=PARAMS,
        cost_estimate=pricing_cost(basis, coef, set_count, owners),
    )(me, *in_hbm(basis, coef, sets, types, gain, lags, limits))


def net_next(me, basis, coef, types, gain, member, like, owners):
    return pl.pallas_call(
        next_net_kernel,
        in_specs=[SCALAR] + [LOCAL] * 5,
        out_specs=LOCAL,
        out_shape=kept(like),
        compiler_params=PARAMS,
        cost_estimate=pricing_cost(basis, coef, member.shape[0], owners),
    )(me, basis, coef, types, gain, member)


def adjoint_kernel(scale, owners, block_paths, me_ref, netted_ref, lags_ref, limits_ref, out_ref):
    rows, set_count = netted_ref.shape
    local_rows = rows // owners
    local_dates = local_rows // block_paths
    dates = owners * local_dates
    lag = lags_ref[...]
    masks = [(lag == value).astype(jnp.float32) for value in range(1, LAG_MAX + 1)]
    places = [
        pl.multiple_of(lax.rem(me_ref[0] + owners - owner, owners) * local_rows, local_rows)
        for owner in range(owners)
    ]
    netted = []
    for place in places:
        block = netted_ref[pl.ds(place, local_rows)]
        netted += [block[i : i + block_paths] for i in range(0, local_rows, block_paths)]
    direct = []
    for date in range(dates):
        collateral = jnp.zeros_like(netted[date])
        for value, mask in enumerate(masks, 1):
            if date >= value:
                collateral = collateral + mask * netted[date - value]
        direct.append(jnp.maximum(netted[date] - collateral - limits_ref[...], 0.0) * scale)
    adjoints = []
    for date in range(dates):
        adjoint = direct[date]
        for value, mask in enumerate(masks, 1):
            if date + value < dates:
                adjoint = adjoint - mask * direct[date + value]
        adjoints.append(adjoint)
    for owner, place in enumerate(places):
        block = jnp.concatenate(adjoints[owner * local_dates : (owner + 1) * local_dates], axis=0)
        block = block.astype(jnp.bfloat16)
        for peer in range(out_ref.shape[0]):
            out_ref[peer, pl.ds(place, local_rows)] = block


def adjoint_of(me, netted, lags, limits, scale, owners, block_paths, peers):
    return pl.pallas_call(
        functools.partial(adjoint_kernel, scale, owners, block_paths),
        in_specs=[SCALAR] + [LOCAL] * 3,
        out_specs=LOCAL,
        out_shape=pltpu.VMEM((peers,) + netted.shape, jnp.bfloat16),
        compiler_params=PARAMS,
    )(me, netted, lags, limits)


def grad_of(member, adjoint_ref, gain, basis):
    peers, rows, set_count = adjoint_ref.shape
    period = gain.shape[1]
    total = None
    together = min(peers, max(1, 512 // rows))
    for first in range(0, peers, together):
        adjoint = adjoint_ref[pl.ds(first, together)].reshape(together * rows, set_count)
        spread = lax.dot_general(member, adjoint, TT, preferred_element_type=jnp.float32)
        scaled = [
            (spread[:, at : at + period] * gain).astype(jnp.bfloat16) for at in range(0, together * rows, period)
        ]
        part = jnp.dot(
            jnp.concatenate(scaled, axis=1),
            basis[first * rows : (first + together) * rows],
            preferred_element_type=jnp.float32,
        )
        total = part if total is None else total + part
    return total


def first_grad_kernel(owners, *refs):
    me_ref, member_ref, adjoint_ref, type_ref = refs[:4]
    gain_refs, basis_refs = refs[4 : 4 + owners], refs[4 + owners : 4 + 2 * owners]
    out_ref, *later_refs = refs[4 + 2 * owners :]
    local_dates, paths, _ = basis_refs[0].shape
    peers, rows, _ = adjoint_ref.shape
    trades, own_depth = out_ref.shape
    local_rows = rows // owners
    block_paths = local_rows // local_dates
    core_paths = peers * block_paths
    me = me_ref[0]
    columns = pl.ds(pl.multiple_of(me * own_depth, own_depth), own_depth)
    orders = [[(step + place) % owners for place in range(owners)] for step in range(owners)]
    basis = []
    for step, order in enumerate(orders):
        sender = lax.rem(me + owners - step, owners)
        at = pl.ds(pl.multiple_of(sender * core_paths, core_paths), core_paths)
        parts = []
        for which in order:
            part = basis_refs[which][:, at, columns].astype(jnp.float32)
            part = part.reshape(local_dates, peers, block_paths, own_depth)
            parts.append(jnp.concatenate([part[date] for date in range(local_dates)], axis=1))
        block = jnp.concatenate(parts, axis=1).reshape(peers * rows, own_depth)
        basis.append(block.astype(jnp.bfloat16))
    period = rows
    while period % 128:
        period *= 2
    dates = owners * local_dates
    rest = jnp.concatenate([gain_of_trades(ref[...], type_ref[...]) for ref in gain_refs], axis=0)
    pieces = []
    for _ in range(3):
        piece = rest.astype(jnp.bfloat16).astype(jnp.float32)
        pieces.append(piece)
        rest = rest - piece
    pieces = jnp.concatenate(pieces, axis=0).astype(jnp.bfloat16)
    lane = lax.broadcasted_iota(jnp.int32, (3 * dates, period), 1)
    have = lax.rem(lax.broadcasted_iota(jnp.int32, (3 * dates, period), 0), dates)
    gain = []
    for step in range(owners):
        want = lax.rem(lax.div(lane, block_paths) + step * local_dates, dates)
        expand = (want == have).astype(jnp.float32).astype(jnp.bfloat16)
        gain.append(lax.dot_general(pieces, expand, TN, preferred_element_type=jnp.float32))
    out_ref[...] = grad_of(member_ref[...], adjoint_ref, gain[0], basis[0])
    for ref, value in zip(later_refs, gain[1:] + basis[1:], strict=True):
        ref[...] = value


def next_grad_kernel(member_ref, adjoint_ref, gain_ref, basis_ref, total_ref, out_ref):
    out_ref[...] = total_ref[...] + grad_of(member_ref[...], adjoint_ref, gain_ref[...], basis_ref[...])


def grad_cost(member, adjoint, own_depth):
    set_count, trades = member.shape
    peers, rows, _ = adjoint.shape
    return pl.CostEstimate(
        flops=2 * trades * peers * rows * (set_count + own_depth),
        bytes_accessed=4 * trades * own_depth,
        transcendentals=0,
    )


def on_device(basis_values, coefficients, set_map, trade_type, type_gain, set_lags, thresholds):
    local_dates, path_count, depth = basis_values.shape
    trades = coefficients.shape[0]
    set_count = thresholds.shape[0]
    peers = lax.axis_size("trades")
    owners = lax.axis_size("dates")
    block_paths = path_count // (peers * owners)
    rows = owners * local_dates * block_paths
    own_depth = depth // owners
    scale = 2.0 / math.sqrt(local_dates * owners * path_count)
    me = lax.axis_index("dates").astype(jnp.int32).reshape(1)

    bases = [shifted(basis_values, "dates", step) for step in range(1, owners)]
    gains = [shifted(type_gain, "dates", step) for step in range(1, owners)]
    partial, member, basis, coef, types, gain, lags, limits = net_first(
        me,
        basis_values,
        coefficients,
        set_map.reshape(1, trades),
        trade_type.reshape(1, trades),
        type_gain,
        set_lags.reshape(1, set_count),
        thresholds.reshape(1, set_count),
        peers,
        owners,
    )
    partials = [partial]
    for other_basis, other_gain in zip(bases, gains, strict=True):
        partials.append(net_next(me, other_basis, coef, types, other_gain, member, partial, owners))
    bases, gains = [basis] + bases, [gain] + gains

    partials = jnp.concatenate(partials, axis=1).astype(jnp.float16)
    arrived = lax.all_to_all(partials, "trades", split_axis=0, concat_axis=0, tiled=True)
    netted = jnp.sum(arrived.astype(jnp.float32), axis=0)
    adjoint = adjoint_of(me, netted, lags, limits, scale, owners, block_paths, peers)
    adjoint = lax.all_to_all(adjoint, "trades", split_axis=0, concat_axis=0, tiled=True)

    adjoints = [adjoint] + [shifted(adjoint, "dates", step) for step in range(1, owners)]
    period = math.lcm(rows, 128)
    later = owners - 1
    total, *ready = pl.pallas_call(
        functools.partial(first_grad_kernel, owners),
        in_specs=[SCALAR] + [LOCAL] * (3 + 2 * owners),
        out_specs=[LOCAL] * (1 + 2 * later),
        out_shape=[pltpu.VMEM((trades, own_depth), jnp.float32)]
        + [pltpu.VMEM((trades, period), jnp.float32)] * later
        + [pltpu.VMEM((peers * rows, own_depth), jnp.bfloat16)] * later,
        compiler_params=PARAMS,
        cost_estimate=grad_cost(member, adjoint, own_depth),
    )(me, member, adjoint, types, *gains, *bases)
    for step in range(later):
        last = step == later - 1
        total = pl.pallas_call(
            next_grad_kernel,
            in_specs=[LOCAL] * 5,
            out_specs=LOCAL,
            out_shape=jax.ShapeDtypeStruct(total.shape, total.dtype) if last else kept(total),
            compiler_params=PARAMS,
            cost_estimate=grad_cost(member, adjoint, own_depth),
        )(member, adjoints[step + 1], ready[step], ready[later + step], total)
    return total


def solution(mesh):
    return jax.shard_map(
        on_device,
        mesh=mesh,
        in_specs=(
            P("dates", "groups", None),
            P("trades", None),
            P("trades"),
            P("trades"),
            P("dates", None),
            P(),
            P(),
        ),
        out_specs=P(("groups", "trades"), "dates"),
        check_vma=False,
    )
```

```python
import functools
import math

import jax
import jax.numpy as jnp
from jax import lax
from jax.experimental import pallas as pl
from jax.experimental.pallas import tpu as pltpu
from jax.sharding import PartitionSpec as P

LAG_MAX = 2
SPAN = 64
NT = (((1,), (1,)), ((), ()))
TN = (((0,), (0,)), ((), ()))
TT = (((0,), (1,)), ((), ()))
PARAMS = pltpu.CompilerParams(vmem_limit_bytes=40 * 1024 * 1024)
SCALAR = pl.BlockSpec(memory_space=pltpu.SMEM)
LOCAL = pl.BlockSpec(memory_space=pltpu.VMEM)


def in_hbm(*arrays):
    return [pltpu.with_memory_space_constraint(array, pltpu.HBM) for array in arrays]


def kept(array):
    return pltpu.VMEM(array.shape, array.dtype)


def shifted(array, axis, step):
    peers = lax.axis_size(axis)
    return lax.ppermute(array, axis, [(i, (i + step) % peers) for i in range(peers)])


def gain_of_trades(gain, types):
    rows = jnp.zeros((gain.shape[0], types.shape[1]), jnp.float32)
    for which in range(gain.shape[1]):
        rows = jnp.where(types == which, gain[:, which : which + 1], rows)
    return rows


def net_paths(me, basis_refs, coef, gain, member, out_ref):
    dates = gain.shape[0]
    depth = coef.shape[1]
    peers, rows, set_count = out_ref.shape
    block_paths = rows // dates
    paths = peers * block_paths
    trades = coef.shape[0]
    span = math.gcd(paths, max(SPAN, block_paths))
    for first in range(0, paths, span):
        at = pl.multiple_of(me * paths + first, span)
        basis = jnp.concatenate([ref[:, pl.ds(at, span), :] for ref in basis_refs], axis=0)
        basis = basis.reshape(dates * span, depth)
        raw = lax.dot_general(basis, coef, NT, preferred_element_type=jnp.float32)
        prices = raw.reshape(dates, span, trades) * gain[:, None, :]
        prices = prices.astype(jnp.bfloat16).reshape(dates * span, trades)
        netted = lax.dot_general(prices, member, NT, preferred_element_type=jnp.float32)
        netted = netted.reshape(dates, span // block_paths, block_paths, set_count)
        for date in range(dates):
            out_ref[
                pl.ds(first // block_paths, span // block_paths), pl.ds(date * block_paths, block_paths)
            ] = netted[date]


def load_kernel(*refs):
    given, (member_ref, gain_rows_ref, *copies), (set_ref, arrived) = refs[:7], refs[7:-2], refs[-2:]
    set_count, trades = member_ref.shape
    type_ref, gain_ref = copies[2:4]
    moves = [
        pltpu.make_async_copy(source, target, arrived.at[at])
        for at, (source, target) in enumerate(zip(given, copies + [set_ref], strict=True))
    ]
    basis_move, coef_move, type_move, gain_move, lags_move, limits_move, set_move = moves
    for move in (set_move, type_move, gain_move, basis_move, coef_move, lags_move, limits_move):
        move.start()
    set_move.wait()
    member = lax.broadcasted_iota(jnp.int32, (set_count, trades), 0) == set_ref[...]
    member_ref[...] = member.astype(jnp.float32).astype(jnp.bfloat16)
    type_move.wait()
    gain_move.wait()
    gain_rows_ref[...] = gain_of_trades(gain_ref[...], type_ref[...])
    basis_move.wait()
    coef_move.wait()
    lags_move.wait()
    limits_move.wait()


def net_kernel(owners, me_ref, coef_ref, type_ref, member_ref, gain_rows_ref, *refs):
    bases, gains, out_ref = refs[:owners], refs[owners:-1], refs[-1]
    rows = [gain_rows_ref[...]] + [gain_of_trades(ref[...], type_ref[...]) for ref in gains]
    net_paths(me_ref[0], bases, coef_ref[...], jnp.concatenate(rows, axis=0), member_ref[...], out_ref)


def load(basis, coef, sets, types, gain, lags, limits):
    trades = coef.shape[0]
    return pl.pallas_call(
        load_kernel,
        in_specs=[pl.BlockSpec(memory_space=pl.ANY)] * 7,
        out_specs=[LOCAL] * 8,
        out_shape=[
            pltpu.VMEM((limits.shape[1], trades), jnp.bfloat16),
            pltpu.VMEM((gain.shape[0], trades), jnp.float32),
        ]
        + [kept(array) for array in (basis, coef, types, gain, lags, limits)],
        scratch_shapes=[pltpu.VMEM(sets.shape, sets.dtype), pltpu.SemaphoreType.DMA((7,))],
        compiler_params=PARAMS,
        cost_estimate=pl.CostEstimate(flops=coef.size * 512, bytes_accessed=coef.size * 2, transcendentals=0),
    )(*in_hbm(basis, coef, types, gain, lags, limits, sets))


def net(me, coef, types, member, gain_rows, bases, later_gains, peers):
    owners = len(bases)
    dates, paths, _ = bases[0].shape
    rows = dates * paths // peers
    return pl.pallas_call(
        functools.partial(net_kernel, owners),
        in_specs=[SCALAR] + [LOCAL] * (3 + 2 * owners),
        out_specs=LOCAL,
        out_shape=pltpu.VMEM((peers, rows, member.shape[0]), jnp.float32),
        compiler_params=PARAMS,
    )(me, coef, types, member, gain_rows, *bases, *later_gains)


def adjoint_kernel(scale, owners, block_paths, me_ref, netted_ref, lags_ref, limits_ref, out_ref):
    rows, set_count = netted_ref.shape
    local_rows = rows // owners
    local_dates = local_rows // block_paths
    dates = owners * local_dates
    lag = lags_ref[...]
    masks = [(lag == value).astype(jnp.float32) for value in range(1, LAG_MAX + 1)]
    places = [
        pl.multiple_of(lax.rem(me_ref[0] + owners - owner, owners) * local_rows, local_rows)
        for owner in range(owners)
    ]
    netted = []
    for place in places:
        block = netted_ref[pl.ds(place, local_rows)]
        netted += [block[i : i + block_paths] for i in range(0, local_rows, block_paths)]
    direct = []
    for date in range(dates):
        collateral = jnp.zeros_like(netted[date])
        for value, mask in enumerate(masks, 1):
            if date >= value:
                collateral = collateral + mask * netted[date - value]
        direct.append(jnp.maximum(netted[date] - collateral - limits_ref[...], 0.0) * scale)
    adjoints = []
    for date in range(dates):
        adjoint = direct[date]
        for value, mask in enumerate(masks, 1):
            if date + value < dates:
                adjoint = adjoint - mask * direct[date + value]
        adjoints.append(adjoint)
    for owner, place in enumerate(places):
        block = jnp.concatenate(adjoints[owner * local_dates : (owner + 1) * local_dates], axis=0)
        block = block.astype(jnp.bfloat16)
        for peer in range(out_ref.shape[0]):
            out_ref[peer, pl.ds(place, local_rows)] = block


def adjoint_of(me, netted, lags, limits, scale, owners, block_paths, peers):
    return pl.pallas_call(
        functools.partial(adjoint_kernel, scale, owners, block_paths),
        in_specs=[SCALAR] + [LOCAL] * 3,
        out_specs=LOCAL,
        out_shape=pltpu.VMEM((peers,) + netted.shape, jnp.bfloat16),
        compiler_params=PARAMS,
    )(me, netted, lags, limits)


def grad_of(member, adjoint_ref, gain, basis):
    peers, rows, set_count = adjoint_ref.shape
    period = gain.shape[1]
    total = None
    together = min(peers, max(1, 512 // rows))
    for first in range(0, peers, together):
        adjoint = adjoint_ref[pl.ds(first, together)].reshape(together * rows, set_count)
        spread = lax.dot_general(member, adjoint, TT, preferred_element_type=jnp.float32)
        scaled = [
            (spread[:, at : at + period] * gain).astype(jnp.bfloat16) for at in range(0, together * rows, period)
        ]
        part = jnp.dot(
            jnp.concatenate(scaled, axis=1),
            basis[first * rows : (first + together) * rows],
            preferred_element_type=jnp.float32,
        )
        total = part if total is None else total + part
    return total


def first_grad_kernel(owners, *refs):
    me_ref, member_ref, adjoint_ref, type_ref = refs[:4]
    gain_refs, basis_refs = refs[4 : 4 + owners], refs[4 + owners : 4 + 2 * owners]
    out_ref, *later_refs = refs[4 + 2 * owners :]
    local_dates, paths, _ = basis_refs[0].shape
    peers, rows, _ = adjoint_ref.shape
    trades, own_depth = out_ref.shape
    local_rows = rows // owners
    block_paths = local_rows // local_dates
    core_paths = peers * block_paths
    me = me_ref[0]
    columns = pl.ds(pl.multiple_of(me * own_depth, own_depth), own_depth)
    orders = [[(step + place) % owners for place in range(owners)] for step in range(owners)]
    basis = []
    for step, order in enumerate(orders):
        sender = lax.rem(me + owners - step, owners)
        at = pl.ds(pl.multiple_of(sender * core_paths, core_paths), core_paths)
        parts = []
        for which in order:
            part = basis_refs[which][:, at, columns].astype(jnp.float32)
            part = part.reshape(local_dates, peers, block_paths, own_depth)
            parts.append(jnp.concatenate([part[date] for date in range(local_dates)], axis=1))
        block = jnp.concatenate(parts, axis=1).reshape(peers * rows, own_depth)
        basis.append(block.astype(jnp.bfloat16))
    period = rows
    while period % 128:
        period *= 2
    dates = owners * local_dates
    rest = jnp.concatenate([gain_of_trades(ref[...], type_ref[...]) for ref in gain_refs], axis=0)
    pieces = []
    for _ in range(3):
        piece = rest.astype(jnp.bfloat16).astype(jnp.float32)
        pieces.append(piece)
        rest = rest - piece
    pieces = jnp.concatenate(pieces, axis=0).astype(jnp.bfloat16)
    lane = lax.broadcasted_iota(jnp.int32, (3 * dates, period), 1)
    have = lax.rem(lax.broadcasted_iota(jnp.int32, (3 * dates, period), 0), dates)
    gain = []
    for step in range(owners):
        want = lax.rem(lax.div(lane, block_paths) + step * local_dates, dates)
        expand = (want == have).astype(jnp.float32).astype(jnp.bfloat16)
        gain.append(lax.dot_general(pieces, expand, TN, preferred_element_type=jnp.float32))
    out_ref[...] = grad_of(member_ref[...], adjoint_ref, gain[0], basis[0])
    for ref, value in zip(later_refs, gain[1:] + basis[1:], strict=True):
        ref[...] = value


def next_grad_kernel(member_ref, adjoint_ref, gain_ref, basis_ref, total_ref, out_ref):
    out_ref[...] = total_ref[...] + grad_of(member_ref[...], adjoint_ref, gain_ref[...], basis_ref[...])


def grad_cost(member, adjoint, own_depth):
    set_count, trades = member.shape
    peers, rows, _ = adjoint.shape
    return pl.CostEstimate(
        flops=2 * trades * peers * rows * (set_count + own_depth),
        bytes_accessed=4 * trades * own_depth,
        transcendentals=0,
    )


def on_device(basis_values, coefficients, set_map, trade_type, type_gain, set_lags, thresholds):
    local_dates, path_count, depth = basis_values.shape
    trades = coefficients.shape[0]
    set_count = thresholds.shape[0]
    peers = lax.axis_size("trades")
    owners = lax.axis_size("dates")
    block_paths = path_count // (peers * owners)
    rows = owners * local_dates * block_paths
    own_depth = depth // owners
    scale = 2.0 / math.sqrt(local_dates * owners * path_count)
    me = lax.axis_index("dates").astype(jnp.int32).reshape(1)

    bases = [shifted(basis_values, "dates", step) for step in range(1, owners)]
    gains = [shifted(type_gain, "dates", step) for step in range(1, owners)]
    member, gain_rows, basis, coef, types, gain, lags, limits = load(
        basis_values,
        coefficients,
        set_map.reshape(1, trades),
        trade_type.reshape(1, trades),
        type_gain,
        set_lags.reshape(1, set_count),
        thresholds.reshape(1, set_count),
    )
    bases, gains = [basis] + bases, [gain] + gains
    partials = net(me, coef, types, member, gain_rows, bases, gains[1:], peers).astype(jnp.float16)
    arrived = lax.all_to_all(partials, "trades", split_axis=0, concat_axis=0, tiled=True)
    netted = jnp.sum(arrived.astype(jnp.float32), axis=0)
    adjoint = adjoint_of(me, netted, lags, limits, scale, owners, block_paths, peers)
    adjoint = lax.all_to_all(adjoint, "trades", split_axis=0, concat_axis=0, tiled=True)

    adjoints = [adjoint] + [shifted(adjoint, "dates", step) for step in range(1, owners)]
    period = math.lcm(rows, 128)
    later = owners - 1
    total, *ready = pl.pallas_call(
        functools.partial(first_grad_kernel, owners),
        in_specs=[SCALAR] + [LOCAL] * (3 + 2 * owners),
        out_specs=[LOCAL] * (1 + 2 * later),
        out_shape=[pltpu.VMEM((trades, own_depth), jnp.float32)]
        + [pltpu.VMEM((trades, period), jnp.float32)] * later
        + [pltpu.VMEM((peers * rows, own_depth), jnp.bfloat16)] * later,
        compiler_params=PARAMS,
        cost_estimate=grad_cost(member, adjoint, own_depth),
    )(me, member, adjoint, types, *gains, *bases)
    for step in range(later):
        last = step == later - 1
        total = pl.pallas_call(
            next_grad_kernel,
            in_specs=[LOCAL] * 5,
            out_specs=LOCAL,
            out_shape=jax.ShapeDtypeStruct(total.shape, total.dtype) if last else kept(total),
            compiler_params=PARAMS,
            cost_estimate=grad_cost(member, adjoint, own_depth),
        )(member, adjoints[step + 1], ready[step], ready[later + step], total)
    return total


def solution(mesh):
    return jax.shard_map(
        on_device,
        mesh=mesh,
        in_specs=(
            P("dates", "groups", None),
            P("trades", None),
            P("trades"),
            P("trades"),
            P("dates", None),
            P(),
            P(),
        ),
        out_specs=P(("groups", "trades"), "dates"),
        check_vma=False,
    )
```

```python
import functools
import math

import jax
import jax.numpy as jnp
from jax import lax
from jax.experimental import pallas as pl
from jax.experimental.pallas import tpu as pltpu
from jax.sharding import PartitionSpec as P

LAG_MAX = 2
ROWS = 512
CUTS = (4,)
ORDER = (0, 2, 1, 3, 7, 5, 4, 6)
NT = (((1,), (1,)), ((), ()))
TN = (((0,), (0,)), ((), ()))
TT = (((0,), (1,)), ((), ()))
PARAMS = pltpu.CompilerParams(vmem_limit_bytes=40 * 1024 * 1024)
SCALAR = pl.BlockSpec(memory_space=pltpu.SMEM)
LOCAL = pl.BlockSpec(memory_space=pltpu.VMEM)


def in_hbm(*arrays):
    return [pltpu.with_memory_space_constraint(array, pltpu.HBM) for array in arrays]


def kept(array):
    return pltpu.VMEM(array.shape, array.dtype)


def rounds_of(peers, owners):
    base = ORDER if peers % len(ORDER) == 0 else range(peers)
    offsets = [first + offset for first in range(0, peers, len(base)) for offset in base]
    assert peers % owners == 0
    return [tuple(offsets[at : at + owners]) for at in range(0, peers, owners)]


def target_of(index, offset, peers):
    return index ^ offset if peers & (peers - 1) == 0 else lax.rem(index + offset, peers)


def source_of(index, offset, peers):
    return index ^ offset if peers & (peers - 1) == 0 else lax.rem(index + (peers - offset), peers)


def offset_at(core, offsets):
    found = jnp.int32(offsets[0])
    for other, offset in enumerate(offsets):
        found = jnp.where(core == other, jnp.int32(offset), found)
    return found


def exchanged(array, offsets, peers):
    owners = len(offsets)
    pairs = [
        (trade * owners + core, int(target_of(trade, offsets[core], peers)) * owners + core)
        for trade in range(peers)
        for core in range(owners)
    ]
    return lax.ppermute(array, ("trades", "dates"), pairs)


def shifted(array, axis, step):
    peers = lax.axis_size(axis)
    return lax.ppermute(array, axis, [(i, (i + step) % peers) for i in range(peers)])


def gain_of_trades(gain, types):
    rows = jnp.zeros((gain.shape[0], types.shape[1]), jnp.float32)
    for which in range(gain.shape[1]):
        rows = jnp.where(types == which, gain[:, which : which + 1], rows)
    return rows


def load_kernel(*refs):
    given, (member_ref, gain_rows_ref, *copies), (set_ref, arrived) = refs[:7], refs[7:-2], refs[-2:]
    set_count, trades = member_ref.shape
    type_ref, gain_ref = copies[2:4]
    moves = [
        pltpu.make_async_copy(source, target, arrived.at[at])
        for at, (source, target) in enumerate(zip(given, copies + [set_ref], strict=True))
    ]
    basis_move, coef_move, type_move, gain_move, lags_move, limits_move, set_move = moves
    for move in (set_move, type_move, gain_move, basis_move, coef_move, lags_move, limits_move):
        move.start()
    set_move.wait()
    member = lax.broadcasted_iota(jnp.int32, (set_count, trades), 0) == set_ref[...]
    member_ref[...] = member.astype(jnp.float32).astype(jnp.bfloat16)
    type_move.wait()
    gain_move.wait()
    gain_rows_ref[...] = gain_of_trades(gain_ref[...], type_ref[...])
    basis_move.wait()
    coef_move.wait()
    lags_move.wait()
    limits_move.wait()


def load(basis, coef, sets, types, gain, lags, limits):
    trades = coef.shape[0]
    return pl.pallas_call(
        load_kernel,
        in_specs=[pl.BlockSpec(memory_space=pl.ANY)] * 7,
        out_specs=[LOCAL] * 8,
        out_shape=[
            pltpu.VMEM((limits.shape[1], trades), jnp.bfloat16),
            pltpu.VMEM((gain.shape[0], trades), jnp.float32),
        ]
        + [kept(array) for array in (basis, coef, types, gain, lags, limits)],
        scratch_shapes=[pltpu.VMEM(sets.shape, sets.dtype), pltpu.SemaphoreType.DMA((7,))],
        compiler_params=PARAMS,
        cost_estimate=pl.CostEstimate(flops=coef.size * 512, bytes_accessed=coef.size * 2, transcendentals=0),
    )(*in_hbm(basis, coef, types, gain, lags, limits, sets))


def net_kernel(rounds, me_ref, trade_ref, coef_ref, type_ref, member_ref, lags_ref, gain_rows_ref, *refs):
    owners = len(rounds[0])
    peers = owners * len(rounds)
    bases, gains, outs = refs[:owners], refs[owners : 2 * owners - 1], refs[2 * owners - 1 :]
    me, trade = me_ref[0], trade_ref[0]
    coef, member, lags = coef_ref[...], member_ref[...], lags_ref[...]
    local_dates, paths, depth = bases[0].shape
    dates = owners * local_dates
    block_paths = paths // peers
    trades, set_count = coef.shape[0], member.shape[0]
    gain = [gain_rows_ref[...]] + [gain_of_trades(ref[...], type_ref[...]) for ref in gains]
    gain = jnp.concatenate(gain, axis=0)
    masks = [(lags == value).astype(jnp.float32) for value in range(1, LAG_MAX + 1)]
    holder = [lax.rem(me + (owners - place), owners) for place in range(owners)]
    earlier = [(owner > 0).astype(jnp.float32) for owner in holder]
    together = max(1, ROWS // (dates * block_paths))
    for first in range(0, len(rounds), together):
        chunk = rounds[first : first + together]
        rows = []
        for offsets in chunk:
            target = target_of(trade, offset_at(me, offsets), peers)
            at = pl.ds(pl.multiple_of(target * block_paths, block_paths), block_paths)
            rows += [ref[:, at, :].reshape(local_dates * block_paths, depth) for ref in bases]
        rows = jnp.concatenate(rows, axis=0)
        raw = lax.dot_general(rows, coef, NT, preferred_element_type=jnp.float32)
        prices = raw.reshape(len(chunk), dates, block_paths, trades) * gain[None, :, None, :]
        prices = prices.astype(jnp.bfloat16).reshape(rows.shape[0], trades)
        netted = lax.dot_general(prices, member, NT, preferred_element_type=jnp.float32)
        netted = netted.reshape(len(chunk), dates, block_paths, set_count)
        for at, out_ref in enumerate(outs[first : first + together]):
            for date in range(dates):
                place, local = divmod(date, local_dates)
                value = netted[at, date]
                for lag, mask in enumerate(masks, 1):
                    if local >= lag:
                        value = value - mask * netted[at, date - lag]
                    else:
                        before = ((place + 1) % owners + 1) * local_dates + local - lag
                        value = value - (mask * earlier[place]) * netted[at, before]
                row = (holder[place] * local_dates + local) * block_paths
                out_ref[pl.ds(pl.multiple_of(row, block_paths), block_paths)] = value


def net(rounds, me, trade, coef, types, member, lags, gain_rows, bases, later_gains):
    owners = len(bases)
    local_dates, paths, _ = bases[0].shape
    rows = local_dates * paths // len(rounds)
    return pl.pallas_call(
        functools.partial(net_kernel, rounds),
        in_specs=[SCALAR] * 2 + [LOCAL] * (4 + 2 * owners),
        out_specs=[LOCAL] * len(rounds),
        out_shape=[pltpu.VMEM((rows, member.shape[0]), jnp.float32)] * len(rounds),
        compiler_params=PARAMS,
    )(me, trade, coef, types, member, lags, gain_rows, *bases, *later_gains)


def adjoint_kernel(scale, block_paths, lags_ref, limits_ref, *refs):
    excess = refs[0][...]
    for ref in refs[1:-1]:
        excess = excess + ref[...]
    rows = excess.shape[0]
    masks = [(lags_ref[...] == value).astype(jnp.float32) for value in range(1, LAG_MAX + 1)]
    direct = jnp.maximum(2.0 * excess - limits_ref[...], 0.0) * scale
    direct = [direct[first : first + block_paths] for first in range(0, rows, block_paths)]
    adjoints = []
    for date, adjoint in enumerate(direct):
        for value, mask in enumerate(masks, 1):
            if date + value < len(direct):
                adjoint = adjoint - mask * direct[date + value]
        adjoints.append(adjoint)
    refs[-1][...] = jnp.concatenate(adjoints, axis=0).astype(jnp.bfloat16)


def adjoint_of(sums, lags, limits, scale, block_paths):
    return pl.pallas_call(
        functools.partial(adjoint_kernel, scale, block_paths),
        in_specs=[LOCAL] * (2 + len(sums)),
        out_specs=LOCAL,
        out_shape=pltpu.VMEM(sums[0].shape, jnp.bfloat16),
        compiler_params=PARAMS,
    )(lags, limits, *sums)


def ready_kernel(rounds, me_ref, trade_ref, type_ref, *refs):
    owners = len(rounds[0])
    peers = owners * len(rounds)
    gain_refs, basis_refs = refs[:owners], refs[owners : 2 * owners]
    gain_ref, *out_refs = refs[2 * owners :]
    local_dates, paths, _ = basis_refs[0].shape
    own_depth = out_refs[0].shape[1]
    block_paths = paths // peers
    local_rows = local_dates * block_paths
    dates = owners * local_dates
    me, trade = me_ref[0], trade_ref[0]
    columns = pl.ds(pl.multiple_of(me * own_depth, own_depth), own_depth)
    for step, out_ref in enumerate(out_refs):
        core = lax.rem(me + (owners - step), owners)
        for at, offsets in enumerate(rounds):
            source = source_of(trade, offset_at(core, offsets), peers)
            span = pl.ds(pl.multiple_of(source * block_paths, block_paths), block_paths)
            for place, ref in enumerate(basis_refs):
                row = at * owners * local_rows + lax.rem(me + (owners - place), owners) * local_rows
                block = ref[:, span, columns].reshape(local_rows, own_depth)
                out_ref[pl.ds(pl.multiple_of(row, local_rows), local_rows)] = block
    rest = jnp.concatenate([gain_of_trades(ref[...], type_ref[...]) for ref in gain_refs], axis=0)
    pieces = []
    for _ in range(3):
        piece = rest.astype(jnp.bfloat16).astype(jnp.float32)
        pieces.append(piece)
        rest = rest - piece
    pieces = jnp.concatenate(pieces, axis=0).astype(jnp.bfloat16)
    shape = (3 * dates, gain_ref.shape[1])
    want = lax.rem(lax.div(lax.broadcasted_iota(jnp.int32, shape, 1), block_paths), dates)
    have = lax.rem(lax.broadcasted_iota(jnp.int32, shape, 0), dates)
    place, local = lax.div(have, local_dates), lax.rem(have, local_dates)
    have = lax.rem(me + owners - place, owners) * local_dates + local
    expand = (want == have).astype(jnp.float32).astype(jnp.bfloat16)
    gain_ref[...] = lax.dot_general(pieces, expand, TN, preferred_element_type=jnp.float32)


def ready(rounds, me, trade, types, gains, bases):
    owners = len(bases)
    local_dates, paths, depth = bases[0].shape
    block_rows = owners * local_dates * paths // (owners * len(rounds))
    rows = block_rows * len(rounds)
    return pl.pallas_call(
        functools.partial(ready_kernel, rounds),
        in_specs=[SCALAR] * 2 + [LOCAL] * (1 + 2 * owners),
        out_specs=[LOCAL] * (1 + owners),
        out_shape=[pltpu.VMEM((types.shape[1], math.lcm(block_rows, 128)), jnp.float32)]
        + [pltpu.VMEM((rows, depth // owners), jnp.bfloat16)] * owners,
        compiler_params=PARAMS,
        cost_estimate=pl.CostEstimate(flops=types.shape[1] * 256 * 1024, bytes_accessed=0, transcendentals=0),
    )(me, trade, types, *gains, *bases)


def grad_kernel(first, carry, member_ref, gain_ref, basis_ref, *refs):
    adjoint_refs, out_ref = refs[carry:-1], refs[-1]
    rows, set_count = adjoint_refs[0].shape
    gain = gain_ref[...]
    period = gain.shape[1]
    member = member_ref[...]
    total = refs[0][...] if carry else None
    together = max(1, ROWS // rows)
    for at in range(0, len(adjoint_refs), together):
        adjoint = jnp.concatenate([ref[...] for ref in adjoint_refs[at : at + together]], axis=0)
        count = adjoint.shape[0]
        spread = lax.dot_general(member, adjoint, TT, preferred_element_type=jnp.float32)
        scaled = [
            (spread[:, left : left + period] * gain).astype(jnp.bfloat16) for left in range(0, count, period)
        ]
        basis = basis_ref[pl.ds((first + at) * rows, count)]
        part = jnp.dot(jnp.concatenate(scaled, axis=1), basis, preferred_element_type=jnp.float32)
        total = part if total is None else total + part
    out_ref[...] = total


def add_grad(total, member, gain, basis, adjoints, first, last):
    carry = int(total is not None)
    trades, own_depth = member.shape[1], basis.shape[1]
    shape = (trades, own_depth)
    count = len(adjoints) * adjoints[0].shape[0]
    return pl.pallas_call(
        functools.partial(grad_kernel, first, carry),
        in_specs=[LOCAL] * (3 + carry + len(adjoints)),
        out_specs=LOCAL,
        out_shape=jax.ShapeDtypeStruct(shape, jnp.float32) if last else pltpu.VMEM(shape, jnp.float32),
        compiler_params=PARAMS,
        cost_estimate=pl.CostEstimate(
            flops=2 * trades * count * (member.shape[0] + own_depth),
            bytes_accessed=4 * trades * own_depth,
            transcendentals=0,
        ),
    )(member, gain, basis, *([total] if carry else []), *adjoints)


def on_device(basis_values, coefficients, set_map, trade_type, type_gain, set_lags, thresholds):
    local_dates, path_count, _ = basis_values.shape
    trades = coefficients.shape[0]
    set_count = thresholds.shape[0]
    peers = lax.axis_size("trades")
    owners = lax.axis_size("dates")
    rounds = rounds_of(peers, owners)
    block_paths = path_count // peers
    scale = 2.0 / math.sqrt(local_dates * owners * path_count)
    me = lax.axis_index("dates").astype(jnp.int32).reshape(1)
    trade = lax.axis_index("trades").astype(jnp.int32).reshape(1)

    bases = [shifted(basis_values, "dates", step) for step in range(1, owners)]
    gains = [shifted(type_gain, "dates", step) for step in range(1, owners)]
    member, gain_rows, basis, coef, types, gain, lags, limits = load(
        basis_values,
        coefficients,
        set_map.reshape(1, trades),
        trade_type.reshape(1, trades),
        type_gain,
        set_lags.reshape(1, set_count),
        thresholds.reshape(1, set_count),
    )
    bases, gains = [basis] + bases, [gain] + gains
    partials = net(rounds, me, trade, coef, types, member, lags, gain_rows, bases, gains[1:])
    arrived = [
        exchanged((partial * 0.5).astype(jnp.float16), offsets, peers)
        for partial, offsets in zip(partials, rounds, strict=True)
    ]
    trade_gain, *basis_rows = ready(rounds, me, trade, types, gains, bases)
    excess = functools.reduce(jnp.add, [part.astype(jnp.float32) for part in arrived])
    excess, trade_gain, *basis_rows = lax.optimization_barrier((excess, trade_gain, *basis_rows))
    sums = [excess] + [shifted(excess, "dates", step) for step in range(1, owners)]
    adjoint = adjoint_of(sums, lags, limits, scale, block_paths)
    adjoints = lax.optimization_barrier([exchanged(adjoint, offsets, peers) for offsets in rounds])

    total = None
    firsts = [0, *(len(rounds) * cut // CUTS[-1] for cut in CUTS[:-1])]
    for first, end in zip(firsts, firsts[1:] + [len(rounds)], strict=True):
        parts = adjoints[first:end]
        if total is not None:
            total, *parts = lax.optimization_barrier((total, *parts))
        swaps = [jnp.stack(parts) if len(parts) > 1 else parts[0]]
        swaps = [shifted(swaps[0], "dates", step) for step in range(1, owners)]
        for step in range(owners):
            if step:
                parts = list(swaps[step - 1]) if len(parts) > 1 else [swaps[step - 1]]
            last = step == owners - 1 and end == len(rounds)
            total = add_grad(total, member, trade_gain, basis_rows[step], parts, first, last)
    return total


def solution(mesh):
    return jax.shard_map(
        on_device,
        mesh=mesh,
        in_specs=(
            P("dates", "groups", None),
            P("trades", None),
            P("trades"),
            P("trades"),
            P("dates", None),
            P(),
            P(),
        ),
        out_specs=P(("groups", "trades"), "dates"),
        check_vma=False,
    )
```

```python
import functools
import math

import jax
import jax.numpy as jnp
from jax import lax
from jax.experimental import pallas as pl
from jax.experimental.pallas import tpu as pltpu
from jax.sharding import PartitionSpec as P

LAG_MAX = 2
ROWS = 512
PIECES = 4
ORDER = (0, 2, 1, 3, 7, 5, 4, 6)
NT = (((1,), (1,)), ((), ()))
TN = (((0,), (0,)), ((), ()))
TT = (((0,), (1,)), ((), ()))
PARAMS = pltpu.CompilerParams(vmem_limit_bytes=40 * 1024 * 1024)
SCALAR = pl.BlockSpec(memory_space=pltpu.SMEM)
LOCAL = pl.BlockSpec(memory_space=pltpu.VMEM)


def in_hbm(*arrays):
    return [pltpu.with_memory_space_constraint(array, pltpu.HBM) for array in arrays]


def kept(array):
    return pltpu.VMEM(array.shape, array.dtype)


def rounds_of(peers, owners):
    base = ORDER if peers % len(ORDER) == 0 else range(peers)
    offsets = [first + offset for first in range(0, peers, len(base)) for offset in base]
    assert peers % owners == 0
    return [tuple(offsets[at : at + owners]) for at in range(0, peers, owners)]


def target_of(index, offset, peers):
    return index ^ offset if peers & (peers - 1) == 0 else lax.rem(index + offset, peers)


def source_of(index, offset, peers):
    return index ^ offset if peers & (peers - 1) == 0 else lax.rem(index + (peers - offset), peers)


def offset_at(core, offsets):
    found = jnp.int32(offsets[0])
    for other, offset in enumerate(offsets):
        found = jnp.where(core == other, jnp.int32(offset), found)
    return found


def exchanged(array, offsets, peers):
    owners = len(offsets)
    pairs = [
        (trade * owners + core, int(target_of(trade, offsets[core], peers)) * owners + core)
        for trade in range(peers)
        for core in range(owners)
    ]
    return lax.ppermute(array, ("trades", "dates"), pairs)


def shifted(array, axis, step):
    peers = lax.axis_size(axis)
    return lax.ppermute(array, axis, [(i, (i + step) % peers) for i in range(peers)])


def gain_of_trades(gain, types):
    rows = jnp.zeros((gain.shape[0], types.shape[1]), jnp.float32)
    for which in range(gain.shape[1]):
        rows = jnp.where(types == which, gain[:, which : which + 1], rows)
    return rows


def load_kernel(*refs):
    given, (member_ref, gain_rows_ref, *copies), (set_ref, arrived) = refs[:7], refs[7:-2], refs[-2:]
    set_count, trades = member_ref.shape
    type_ref, gain_ref = copies[2:4]
    moves = [
        pltpu.make_async_copy(source, target, arrived.at[at])
        for at, (source, target) in enumerate(zip(given, copies + [set_ref], strict=True))
    ]
    basis_move, coef_move, type_move, gain_move, lags_move, limits_move, set_move = moves
    for move in (set_move, type_move, gain_move, basis_move, coef_move, lags_move, limits_move):
        move.start()
    set_move.wait()
    member = lax.broadcasted_iota(jnp.int32, (set_count, trades), 0) == set_ref[...]
    member_ref[...] = member.astype(jnp.float32).astype(jnp.bfloat16)
    type_move.wait()
    gain_move.wait()
    gain_rows_ref[...] = gain_of_trades(gain_ref[...], type_ref[...])
    basis_move.wait()
    coef_move.wait()
    lags_move.wait()
    limits_move.wait()


def load(basis, coef, sets, types, gain, lags, limits):
    trades = coef.shape[0]
    return pl.pallas_call(
        load_kernel,
        in_specs=[pl.BlockSpec(memory_space=pl.ANY)] * 7,
        out_specs=[LOCAL] * 8,
        out_shape=[
            pltpu.VMEM((limits.shape[1], trades), jnp.bfloat16),
            pltpu.VMEM((gain.shape[0], trades), jnp.float32),
        ]
        + [kept(array) for array in (basis, coef, types, gain, lags, limits)],
        scratch_shapes=[pltpu.VMEM(sets.shape, sets.dtype), pltpu.SemaphoreType.DMA((7,))],
        compiler_params=PARAMS,
        cost_estimate=pl.CostEstimate(flops=coef.size * 512, bytes_accessed=coef.size * 2, transcendentals=0),
    )(*in_hbm(basis, coef, types, gain, lags, limits, sets))


def net_kernel(rounds, me_ref, trade_ref, coef_ref, type_ref, member_ref, lags_ref, gain_rows_ref, *refs):
    owners = len(rounds[0])
    peers = owners * len(rounds)
    bases, gains, outs = refs[:owners], refs[owners : 2 * owners - 1], refs[2 * owners - 1 :]
    me, trade = me_ref[0], trade_ref[0]
    coef, member, lags = coef_ref[...], member_ref[...], lags_ref[...]
    local_dates, paths, depth = bases[0].shape
    dates = owners * local_dates
    block_paths = paths // peers
    trades, set_count = coef.shape[0], member.shape[0]
    gain = [gain_rows_ref[...]] + [gain_of_trades(ref[...], type_ref[...]) for ref in gains]
    gain = jnp.concatenate(gain, axis=0)
    masks = [(lags == value).astype(jnp.float32) for value in range(1, LAG_MAX + 1)]
    holder = [lax.rem(me + (owners - place), owners) for place in range(owners)]
    earlier = [(owner > 0).astype(jnp.float32) for owner in holder]
    together = max(1, ROWS // (dates * block_paths))
    for first in range(0, len(rounds), together):
        chunk = rounds[first : first + together]
        rows = []
        for offsets in chunk:
            target = target_of(trade, offset_at(me, offsets), peers)
            at = pl.ds(pl.multiple_of(target * block_paths, block_paths), block_paths)
            rows += [ref[:, at, :].reshape(local_dates * block_paths, depth) for ref in bases]
        rows = jnp.concatenate(rows, axis=0)
        raw = lax.dot_general(rows, coef, NT, preferred_element_type=jnp.float32)
        prices = raw.reshape(len(chunk), dates, block_paths, trades) * gain[None, :, None, :]
        prices = prices.astype(jnp.bfloat16).reshape(rows.shape[0], trades)
        netted = lax.dot_general(prices, member, NT, preferred_element_type=jnp.float32)
        netted = netted.reshape(len(chunk), dates, block_paths, set_count)
        for at, out_ref in enumerate(outs[first : first + together]):
            for date in range(dates):
                place, local = divmod(date, local_dates)
                value = netted[at, date]
                for lag, mask in enumerate(masks, 1):
                    if local >= lag:
                        value = value - mask * netted[at, date - lag]
                    else:
                        before = ((place + 1) % owners + 1) * local_dates + local - lag
                        value = value - (mask * earlier[place]) * netted[at, before]
                row = (holder[place] * local_dates + local) * block_paths
                out_ref[pl.ds(pl.multiple_of(row, block_paths), block_paths)] = value


def net(rounds, me, trade, coef, types, member, lags, gain_rows, bases, later_gains):
    owners = len(bases)
    local_dates, paths, _ = bases[0].shape
    rows = local_dates * paths // len(rounds)
    return pl.pallas_call(
        functools.partial(net_kernel, rounds),
        in_specs=[SCALAR] * 2 + [LOCAL] * (4 + 2 * owners),
        out_specs=[LOCAL] * len(rounds),
        out_shape=[pltpu.VMEM((rows, member.shape[0]), jnp.float32)] * len(rounds),
        compiler_params=PARAMS,
    )(me, trade, coef, types, member, lags, gain_rows, *bases, *later_gains)


def adjoint_kernel(scale, block_paths, lags_ref, limits_ref, *refs):
    excess = refs[0][...]
    for ref in refs[1:-1]:
        excess = excess + ref[...]
    rows = excess.shape[0]
    masks = [(lags_ref[...] == value).astype(jnp.float32) for value in range(1, LAG_MAX + 1)]
    direct = jnp.maximum(2.0 * excess - limits_ref[...], 0.0) * scale
    direct = [direct[first : first + block_paths] for first in range(0, rows, block_paths)]
    adjoints = []
    for date, adjoint in enumerate(direct):
        for value, mask in enumerate(masks, 1):
            if date + value < len(direct):
                adjoint = adjoint - mask * direct[date + value]
        adjoints.append(adjoint)
    refs[-1][...] = jnp.concatenate(adjoints, axis=0).astype(jnp.bfloat16)


def adjoint_of(sums, lags, limits, scale, block_paths):
    return pl.pallas_call(
        functools.partial(adjoint_kernel, scale, block_paths),
        in_specs=[LOCAL] * (2 + len(sums)),
        out_specs=LOCAL,
        out_shape=pltpu.VMEM(sums[0].shape, jnp.bfloat16),
        compiler_params=PARAMS,
    )(lags, limits, *sums)


def ready_kernel(rounds, me_ref, trade_ref, type_ref, *refs):
    owners = len(rounds[0])
    peers = owners * len(rounds)
    gain_refs, basis_refs = refs[:owners], refs[owners : 2 * owners]
    gain_ref, *out_refs = refs[2 * owners :]
    local_dates, paths, _ = basis_refs[0].shape
    own_depth = out_refs[0].shape[1]
    block_paths = paths // peers
    local_rows = local_dates * block_paths
    dates = owners * local_dates
    me, trade = me_ref[0], trade_ref[0]
    columns = pl.ds(pl.multiple_of(me * own_depth, own_depth), own_depth)
    for step, out_ref in enumerate(out_refs):
        core = lax.rem(me + (owners - step), owners)
        for at, offsets in enumerate(rounds):
            source = source_of(trade, offset_at(core, offsets), peers)
            span = pl.ds(pl.multiple_of(source * block_paths, block_paths), block_paths)
            for place, ref in enumerate(basis_refs):
                row = at * owners * local_rows + lax.rem(me + (owners - place), owners) * local_rows
                block = ref[:, span, columns].reshape(local_rows, own_depth)
                out_ref[pl.ds(pl.multiple_of(row, local_rows), local_rows)] = block
    rest = jnp.concatenate([gain_of_trades(ref[...], type_ref[...]) for ref in gain_refs], axis=0)
    pieces = []
    for _ in range(3):
        piece = rest.astype(jnp.bfloat16).astype(jnp.float32)
        pieces.append(piece)
        rest = rest - piece
    pieces = jnp.concatenate(pieces, axis=0).astype(jnp.bfloat16)
    shape = (3 * dates, gain_ref.shape[1])
    want = lax.rem(lax.div(lax.broadcasted_iota(jnp.int32, shape, 1), block_paths), dates)
    have = lax.rem(lax.broadcasted_iota(jnp.int32, shape, 0), dates)
    place, local = lax.div(have, local_dates), lax.rem(have, local_dates)
    have = lax.rem(me + owners - place, owners) * local_dates + local
    expand = (want == have).astype(jnp.float32).astype(jnp.bfloat16)
    gain_ref[...] = lax.dot_general(pieces, expand, TN, preferred_element_type=jnp.float32)


def ready(rounds, me, trade, types, gains, bases):
    owners = len(bases)
    local_dates, paths, depth = bases[0].shape
    block_rows = owners * local_dates * paths // (owners * len(rounds))
    rows = block_rows * len(rounds)
    return pl.pallas_call(
        functools.partial(ready_kernel, rounds),
        in_specs=[SCALAR] * 2 + [LOCAL] * (1 + 2 * owners),
        out_specs=[LOCAL] * (1 + owners),
        out_shape=[pltpu.VMEM((types.shape[1], math.lcm(block_rows, 128)), jnp.float32)]
        + [pltpu.VMEM((rows, depth // owners), jnp.bfloat16)] * owners,
        compiler_params=PARAMS,
        cost_estimate=pl.CostEstimate(flops=types.shape[1] * 256 * 1024, bytes_accessed=0, transcendentals=0),
    )(me, trade, types, *gains, *bases)


def grad_kernel(carry, last, member_ref, gain_ref, basis_ref, *refs):
    out_ref, *scratch = refs[-3:] if last else refs[-1:]
    adjoint_refs = refs[carry : -3 if last else -1]
    rows, set_count = adjoint_refs[0].shape
    trades = member_ref.shape[1]
    gain = gain_ref[...]
    period = gain.shape[1]
    member = member_ref[...]
    total = refs[0][...] if carry else None
    together = max(1, ROWS // rows)
    for at in range(0, len(adjoint_refs), together):
        adjoint = jnp.concatenate([ref[...] for ref in adjoint_refs[at : at + together]], axis=0)
        count = adjoint.shape[0]
        spread = lax.dot_general(member, adjoint, TT, preferred_element_type=jnp.float32)
        scaled = [
            (spread[:, left : left + period] * gain).astype(jnp.bfloat16) for left in range(0, count, period)
        ]
        scaled = jnp.concatenate(scaled, axis=1)
        basis = basis_ref[pl.ds(at * rows, count)]
        if last and at + together >= len(adjoint_refs):
            sum_ref, written = scratch
            size = trades // written.shape[0]
            moves = []
            for piece in range(written.shape[0]):
                span = pl.ds(piece * size, size)
                left, right = piece * size, (piece + 1) * size
                part = jnp.dot(scaled[left:right], basis, preferred_element_type=jnp.float32)
                sum_ref[span] = part if total is None else total[left:right] + part
                moves.append(pltpu.make_async_copy(sum_ref.at[span], out_ref.at[span], written.at[piece]))
                moves[-1].start()
            for move in moves:
                move.wait()
            return
        part = jnp.dot(scaled, basis, preferred_element_type=jnp.float32)
        total = part if total is None else total + part
    out_ref[...] = total


def add_grad(total, member, gain, basis, adjoints, last):
    carry = int(total is not None)
    trades, own_depth = member.shape[1], basis.shape[1]
    shape = (trades, own_depth)
    count = len(adjoints) * adjoints[0].shape[0]
    pieces = math.gcd(trades // 128, PIECES) if trades % 128 == 0 else 1
    return pl.pallas_call(
        functools.partial(grad_kernel, carry, last),
        in_specs=[LOCAL] * (3 + carry + len(adjoints)),
        out_specs=pl.BlockSpec(memory_space=pl.ANY) if last else LOCAL,
        out_shape=jax.ShapeDtypeStruct(shape, jnp.float32) if last else pltpu.VMEM(shape, jnp.float32),
        scratch_shapes=[pltpu.VMEM(shape, jnp.float32), pltpu.SemaphoreType.DMA((pieces,))] if last else [],
        compiler_params=PARAMS,
        cost_estimate=pl.CostEstimate(
            flops=2 * trades * count * (member.shape[0] + own_depth),
            bytes_accessed=4 * trades * own_depth,
            transcendentals=0,
        ),
    )(member, gain, basis, *([total] if carry else []), *adjoints)


def on_device(basis_values, coefficients, set_map, trade_type, type_gain, set_lags, thresholds):
    local_dates, path_count, _ = basis_values.shape
    trades = coefficients.shape[0]
    set_count = thresholds.shape[0]
    peers = lax.axis_size("trades")
    owners = lax.axis_size("dates")
    rounds = rounds_of(peers, owners)
    block_paths = path_count // peers
    scale = 2.0 / math.sqrt(local_dates * owners * path_count)
    me = lax.axis_index("dates").astype(jnp.int32).reshape(1)
    trade = lax.axis_index("trades").astype(jnp.int32).reshape(1)

    bases = [shifted(basis_values, "dates", step) for step in range(1, owners)]
    gains = [shifted(type_gain, "dates", step) for step in range(1, owners)]
    member, gain_rows, basis, coef, types, gain, lags, limits = load(
        basis_values,
        coefficients,
        set_map.reshape(1, trades),
        trade_type.reshape(1, trades),
        type_gain,
        set_lags.reshape(1, set_count),
        thresholds.reshape(1, set_count),
    )
    bases, gains = [basis] + bases, [gain] + gains
    partials = net(rounds, me, trade, coef, types, member, lags, gain_rows, bases, gains[1:])
    arrived = [
        exchanged((partial * 0.5).astype(jnp.float16), offsets, peers)
        for partial, offsets in zip(partials, rounds, strict=True)
    ]
    trade_gain, *basis_rows = ready(rounds, me, trade, types, gains, bases)
    excess = functools.reduce(jnp.add, [part.astype(jnp.float32) for part in arrived])
    excess, trade_gain, *basis_rows = lax.optimization_barrier((excess, trade_gain, *basis_rows))
    sums = [excess] + [shifted(excess, "dates", step) for step in range(1, owners)]
    adjoint = adjoint_of(sums, lags, limits, scale, block_paths)
    adjoints = lax.optimization_barrier([exchanged(adjoint, offsets, peers) for offsets in rounds])

    block = jnp.stack(adjoints)
    total = None
    for step in range(owners):
        there = list(shifted(block, "dates", step)) if step else adjoints
        total = add_grad(total, member, trade_gain, basis_rows[step], there, step == owners - 1)
    return total


def solution(mesh):
    return jax.shard_map(
        on_device,
        mesh=mesh,
        in_specs=(
            P("dates", "groups", None),
            P("trades", None),
            P("trades"),
            P("trades"),
            P("dates", None),
            P(),
            P(),
        ),
        out_specs=P(("groups", "trades"), "dates"),
        check_vma=False,
    )
```

```python
import functools
import math

import jax
import jax.numpy as jnp
from jax import lax
from jax.experimental import pallas as pl
from jax.experimental.pallas import tpu as pltpu
from jax.sharding import PartitionSpec as P

LAG_MAX = 2
ROWS = 1024
PIECES = 4
ORDER_IN = (0, 2, 1, 3, 7, 5, 4, 6)
ORDER_OUT = (0, 1, 2, 3, 7, 6, 4, 5)
NT = (((1,), (1,)), ((), ()))
TN = (((0,), (0,)), ((), ()))
TT = (((0,), (1,)), ((), ()))
PARAMS = pltpu.CompilerParams(vmem_limit_bytes=40 * 1024 * 1024)
SCALAR = pl.BlockSpec(memory_space=pltpu.SMEM)
LOCAL = pl.BlockSpec(memory_space=pltpu.VMEM)


def in_hbm(*arrays):
    return [pltpu.with_memory_space_constraint(array, pltpu.HBM) for array in arrays]


def kept(array):
    return pltpu.VMEM(array.shape, array.dtype)


def offsets_of(order, peers):
    base = order if peers % len(order) == 0 else range(peers)
    return [first + offset for first in range(0, peers, len(base)) for offset in base]


def rounds_of(offsets, owners):
    assert len(offsets) % owners == 0
    return [tuple(offsets[at : at + owners]) for at in range(0, len(offsets), owners)]


def shared_of(peers, owners):
    return range(1, 1 + (peers - 1) % owners)


def target_of(index, offset, peers):
    return index ^ offset if peers & (peers - 1) == 0 else lax.rem(index + offset, peers)


def source_of(index, offset, peers):
    return index ^ offset if peers & (peers - 1) == 0 else lax.rem(index + (peers - offset), peers)


def offset_at(core, offsets):
    found = jnp.int32(offsets[0])
    for other, offset in enumerate(offsets):
        found = jnp.where(core == other, jnp.int32(offset), found)
    return found


def exchanged(array, offsets, peers):
    owners = len(offsets)
    pairs = [
        (trade * owners + core, int(target_of(trade, offsets[core], peers)) * owners + core)
        for trade in range(peers)
        for core in range(owners)
    ]
    return lax.ppermute(array, ("trades", "dates"), pairs)


def together_kernel(count, *refs):
    for at in range(count):
        refs[-1][at] = refs[at - 1 - count][...]


def together_of(arrays, others):
    shape = (len(arrays),) + arrays[0].shape
    return pl.pallas_call(
        functools.partial(together_kernel, len(arrays)),
        in_specs=[LOCAL] * (len(arrays) + len(others)),
        out_specs=LOCAL,
        out_shape=pltpu.VMEM(shape, arrays[0].dtype),
        compiler_params=PARAMS,
    )(*others, *arrays)


def shifted(array, axis, step):
    peers = lax.axis_size(axis)
    return lax.ppermute(array, axis, [(i, (i + step) % peers) for i in range(peers)])


def gain_of_trades(gain, types):
    rows = jnp.zeros((gain.shape[0], types.shape[1]), jnp.float32)
    for which in range(gain.shape[1]):
        rows = jnp.where(types == which, gain[:, which : which + 1], rows)
    return rows


def load_kernel(*refs):
    given, (member_ref, gain_rows_ref, *copies), (set_ref, arrived) = refs[:7], refs[7:-2], refs[-2:]
    set_count, trades = member_ref.shape
    type_ref, gain_ref = copies[2:4]
    moves = [
        pltpu.make_async_copy(source, target, arrived.at[at])
        for at, (source, target) in enumerate(zip(given, copies + [set_ref], strict=True))
    ]
    basis_move, coef_move, type_move, gain_move, lags_move, limits_move, set_move = moves
    for move in (set_move, type_move, gain_move, basis_move, coef_move, lags_move, limits_move):
        move.start()
    set_move.wait()
    member = lax.broadcasted_iota(jnp.int32, (set_count, trades), 0) == set_ref[...]
    member_ref[...] = member.astype(jnp.float32).astype(jnp.bfloat16)
    type_move.wait()
    gain_move.wait()
    gain_rows_ref[...] = gain_of_trades(gain_ref[...], type_ref[...])
    basis_move.wait()
    coef_move.wait()
    lags_move.wait()
    limits_move.wait()


def load(basis, coef, sets, types, gain, lags, limits):
    trades = coef.shape[0]
    return pl.pallas_call(
        load_kernel,
        in_specs=[pl.BlockSpec(memory_space=pl.ANY)] * 7,
        out_specs=[LOCAL] * 8,
        out_shape=[
            pltpu.VMEM((limits.shape[1], trades), jnp.bfloat16),
            pltpu.VMEM((gain.shape[0], trades), jnp.float32),
        ]
        + [kept(array) for array in (basis, coef, types, gain, lags, limits)],
        scratch_shapes=[pltpu.VMEM(sets.shape, sets.dtype), pltpu.SemaphoreType.DMA((7,))],
        compiler_params=PARAMS,
        cost_estimate=pl.CostEstimate(flops=coef.size * 512, bytes_accessed=coef.size * 2, transcendentals=0),
    )(*in_hbm(basis, coef, types, gain, lags, limits, sets))


def net_kernel(rounds, peers, me_ref, trade_ref, coef_ref, type_ref, member_ref, lags_ref, gain_rows_ref, *refs):
    owners = len(rounds[0])
    bases, gains, outs = refs[:owners], refs[owners : 2 * owners - 1], refs[2 * owners - 1 :]
    me, trade = me_ref[0], trade_ref[0]
    coef, member, lags = coef_ref[...], member_ref[...], lags_ref[...]
    local_dates, paths, depth = bases[0].shape
    dates = owners * local_dates
    block_paths = paths // peers
    trades, set_count = coef.shape[0], member.shape[0]
    gain = [gain_rows_ref[...]] + [gain_of_trades(ref[...], type_ref[...]) for ref in gains]
    gain = jnp.concatenate(gain, axis=0)
    masks = [(lags == value).astype(jnp.float32) for value in range(1, LAG_MAX + 1)]
    holder = [lax.rem(me + (owners - place), owners) for place in range(owners)]
    earlier = [(owner > 0).astype(jnp.float32) for owner in holder]
    together = max(1, ROWS // (dates * block_paths))
    for first in range(0, len(rounds), together):
        chunk = rounds[first : first + together]
        rows = []
        for offsets in chunk:
            target = target_of(trade, offset_at(me, offsets), peers)
            at = pl.ds(pl.multiple_of(target * block_paths, block_paths), block_paths)
            rows += [ref[:, at, :].reshape(local_dates * block_paths, depth) for ref in bases]
        rows = jnp.concatenate(rows, axis=0)
        raw = lax.dot_general(rows, coef, NT, preferred_element_type=jnp.float32)
        prices = raw.reshape(len(chunk), dates, block_paths, trades) * gain[None, :, None, :]
        prices = prices.astype(jnp.bfloat16).reshape(rows.shape[0], trades)
        netted = lax.dot_general(prices, member, NT, preferred_element_type=jnp.float32)
        netted = netted.reshape(len(chunk), dates, block_paths, set_count)
        for at, out_ref in enumerate(outs[first : first + together]):
            for date in range(dates):
                place, local = divmod(date, local_dates)
                value = netted[at, date]
                for lag, mask in enumerate(masks, 1):
                    if local >= lag:
                        value = value - mask * netted[at, date - lag]
                    else:
                        before = ((place + 1) % owners + 1) * local_dates + local - lag
                        value = value - (mask * earlier[place]) * netted[at, before]
                row = (holder[place] * local_dates + local) * block_paths
                out_ref[pl.ds(pl.multiple_of(row, block_paths), block_paths)] = value


def net(rounds, peers, me, trade, coef, types, member, lags, gain_rows, bases, later_gains):
    owners = len(bases)
    local_dates, paths, _ = bases[0].shape
    rows = owners * local_dates * paths // peers
    return pl.pallas_call(
        functools.partial(net_kernel, rounds, peers),
        in_specs=[SCALAR] * 2 + [LOCAL] * (4 + 2 * owners),
        out_specs=[LOCAL] * len(rounds),
        out_shape=[pltpu.VMEM((rows, member.shape[0]), jnp.float32)] * len(rounds),
        compiler_params=PARAMS,
    )(me, trade, coef, types, member, lags, gain_rows, *bases, *later_gains)


def adjoint_kernel(scale, block_paths, lags_ref, limits_ref, *refs):
    excess = refs[0][...]
    for ref in refs[1:-1]:
        excess = excess + ref[...]
    rows = excess.shape[0]
    masks = [(lags_ref[...] == value).astype(jnp.float32) for value in range(1, LAG_MAX + 1)]
    direct = jnp.maximum(2.0 * excess - limits_ref[...], 0.0) * scale
    direct = [direct[first : first + block_paths] for first in range(0, rows, block_paths)]
    adjoints = []
    for date, adjoint in enumerate(direct):
        for value, mask in enumerate(masks, 1):
            if date + value < len(direct):
                adjoint = adjoint - mask * direct[date + value]
        adjoints.append(adjoint)
    refs[-1][...] = jnp.concatenate(adjoints, axis=0).astype(jnp.bfloat16)


def adjoint_of(sums, lags, limits, scale, block_paths):
    return pl.pallas_call(
        functools.partial(adjoint_kernel, scale, block_paths),
        in_specs=[LOCAL] * (2 + len(sums)),
        out_specs=LOCAL,
        out_shape=pltpu.VMEM(sums[0].shape, jnp.bfloat16),
        compiler_params=PARAMS,
    )(lags, limits, *sums)


def ready_kernel(rounds, near, peers, me_ref, trade_ref, type_ref, *refs):
    owners = len(rounds[0])
    gain_refs, basis_refs = refs[:owners], refs[owners : 2 * owners]
    gain_ref, *out_refs = refs[2 * owners :]
    local_dates, paths, _ = basis_refs[0].shape
    own_depth = out_refs[0].shape[1]
    block_paths = paths // peers
    local_rows = local_dates * block_paths
    dates = owners * local_dates
    me, trade = me_ref[0], trade_ref[0]
    columns = pl.ds(pl.multiple_of(me * own_depth, own_depth), own_depth)
    for step, out_ref in enumerate(out_refs):
        core = lax.rem(me + (owners - step), owners)
        for at, offsets in enumerate(rounds if step else near + rounds):
            source = source_of(trade, offset_at(core, offsets), peers)
            span = pl.ds(pl.multiple_of(source * block_paths, block_paths), block_paths)
            for place, ref in enumerate(basis_refs):
                row = at * owners * local_rows + lax.rem(me + (owners - place), owners) * local_rows
                block = ref[:, span, columns].reshape(local_rows, own_depth)
                out_ref[pl.ds(pl.multiple_of(row, local_rows), local_rows)] = block
    rest = jnp.concatenate([gain_of_trades(ref[...], type_ref[...]) for ref in gain_refs], axis=0)
    pieces = []
    for _ in range(3):
        piece = rest.astype(jnp.bfloat16).astype(jnp.float32)
        pieces.append(piece)
        rest = rest - piece
    pieces = jnp.concatenate(pieces, axis=0).astype(jnp.bfloat16)
    shape = (3 * dates, gain_ref.shape[1])
    want = lax.rem(lax.div(lax.broadcasted_iota(jnp.int32, shape, 1), block_paths), dates)
    have = lax.rem(lax.broadcasted_iota(jnp.int32, shape, 0), dates)
    place, local = lax.div(have, local_dates), lax.rem(have, local_dates)
    have = lax.rem(me + owners - place, owners) * local_dates + local
    expand = (want == have).astype(jnp.float32).astype(jnp.bfloat16)
    gain_ref[...] = lax.dot_general(pieces, expand, TN, preferred_element_type=jnp.float32)


def ready(rounds, near, peers, me, trade, types, gains, bases):
    owners = len(bases)
    local_dates, paths, depth = bases[0].shape
    block_rows = owners * local_dates * paths // peers
    counts = [len(rounds) + len(near)] + [len(rounds)] * (owners - 1)
    return pl.pallas_call(
        functools.partial(ready_kernel, rounds, near, peers),
        in_specs=[SCALAR] * 2 + [LOCAL] * (1 + 2 * owners),
        out_specs=[LOCAL] * (1 + owners),
        out_shape=[pltpu.VMEM((types.shape[1], math.lcm(block_rows, 128)), jnp.float32)]
        + [pltpu.VMEM((block_rows * count, depth // owners), jnp.bfloat16) for count in counts],
        compiler_params=PARAMS,
        cost_estimate=pl.CostEstimate(flops=types.shape[1] * 256 * 1024, bytes_accessed=0, transcendentals=0),
    )(me, trade, types, *gains, *bases)


def grad_kernel(carry, last, member_ref, gain_ref, basis_ref, *refs):
    out_ref, *scratch = refs[-3:] if last else refs[-1:]
    adjoint_refs = refs[carry : -3 if last else -1]
    rows, set_count = adjoint_refs[0].shape
    trades = member_ref.shape[1]
    gain = gain_ref[...]
    period = gain.shape[1]
    member = member_ref[...]
    total = refs[0][...] if carry else None
    together = max(1, ROWS // rows)
    for at in range(0, len(adjoint_refs), together):
        adjoint = jnp.concatenate([ref[...] for ref in adjoint_refs[at : at + together]], axis=0)
        count = adjoint.shape[0]
        spread = lax.dot_general(member, adjoint, TT, preferred_element_type=jnp.float32)
        scaled = [
            (spread[:, left : left + period] * gain).astype(jnp.bfloat16) for left in range(0, count, period)
        ]
        scaled = jnp.concatenate(scaled, axis=1)
        basis = basis_ref[pl.ds(at * rows, count)]
        if last and at + together >= len(adjoint_refs):
            sum_ref, written = scratch
            size = trades // written.shape[0]
            moves = []
            for piece in range(written.shape[0]):
                span = pl.ds(piece * size, size)
                left, right = piece * size, (piece + 1) * size
                part = jnp.dot(scaled[left:right], basis, preferred_element_type=jnp.float32)
                sum_ref[span] = part if total is None else total[left:right] + part
                moves.append(pltpu.make_async_copy(sum_ref.at[span], out_ref.at[span], written.at[piece]))
                moves[-1].start()
            for move in moves:
                move.wait()
            return
        part = jnp.dot(scaled, basis, preferred_element_type=jnp.float32)
        total = part if total is None else total + part
    out_ref[...] = total


def add_grad(total, member, gain, basis, adjoints, last):
    carry = int(total is not None)
    trades, own_depth = member.shape[1], basis.shape[1]
    shape = (trades, own_depth)
    count = len(adjoints) * adjoints[0].shape[0]
    pieces = math.gcd(trades // 128, PIECES) if trades % 128 == 0 else 1
    return pl.pallas_call(
        functools.partial(grad_kernel, carry, last),
        in_specs=[LOCAL] * (3 + carry + len(adjoints)),
        out_specs=pl.BlockSpec(memory_space=pl.ANY) if last else LOCAL,
        out_shape=jax.ShapeDtypeStruct(shape, jnp.float32) if last else pltpu.VMEM(shape, jnp.float32),
        scratch_shapes=[pltpu.VMEM(shape, jnp.float32), pltpu.SemaphoreType.DMA((pieces,))] if last else [],
        compiler_params=PARAMS,
        cost_estimate=pl.CostEstimate(
            flops=2 * trades * count * (member.shape[0] + own_depth),
            bytes_accessed=4 * trades * own_depth,
            transcendentals=0,
        ),
    )(member, gain, basis, *([total] if carry else []), *adjoints)


def on_device(basis_values, coefficients, set_map, trade_type, type_gain, set_lags, thresholds):
    local_dates, path_count, _ = basis_values.shape
    trades = coefficients.shape[0]
    set_count = thresholds.shape[0]
    peers = lax.axis_size("trades")
    owners = lax.axis_size("dates")
    rounds_in = rounds_of(offsets_of(ORDER_IN, peers), owners)
    shared = shared_of(peers, owners)
    rounds_out = [offset for offset in offsets_of(ORDER_OUT, peers) if offset > len(shared)]
    rounds_out = rounds_of(rounds_out, owners)
    near = [(offset,) * owners for offset in shared]
    block_paths = path_count // peers
    scale = 2.0 / math.sqrt(local_dates * owners * path_count)
    me = lax.axis_index("dates").astype(jnp.int32).reshape(1)
    trade = lax.axis_index("trades").astype(jnp.int32).reshape(1)

    bases = [shifted(basis_values, "dates", step) for step in range(1, owners)]
    gains = [shifted(type_gain, "dates", step) for step in range(1, owners)]
    member, gain_rows, basis, coef, types, gain, lags, limits = load(
        basis_values,
        coefficients,
        set_map.reshape(1, trades),
        trade_type.reshape(1, trades),
        type_gain,
        set_lags.reshape(1, set_count),
        thresholds.reshape(1, set_count),
    )
    bases, gains = [basis] + bases, [gain] + gains
    partials = net(rounds_in, peers, me, trade, coef, types, member, lags, gain_rows, bases, gains[1:])
    arrived = [
        exchanged((partial * 0.5).astype(jnp.float16), offsets, peers)
        for partial, offsets in zip(partials, rounds_in, strict=True)
    ]
    trade_gain, *basis_rows = ready(rounds_out, near + [(0,) * owners], peers, me, trade, types, gains, bases)
    excess = functools.reduce(jnp.add, [part.astype(jnp.float32) for part in arrived])
    excess, trade_gain, *basis_rows = lax.optimization_barrier((excess, trade_gain, *basis_rows))
    sums = [excess] + [shifted(excess, "dates", step) for step in range(1, owners)]
    adjoint = adjoint_of(sums, lags, limits, scale, block_paths)
    close = [exchanged(adjoint, offsets, peers) for offsets in near] + [adjoint]
    apart = [exchanged(adjoint, offsets, peers) for offsets in rounds_out]
    whole = together_of(apart, close)
    total = add_grad(None, member, trade_gain, basis_rows[0], close + apart, False)
    for step in range(1, owners):
        there = list(shifted(whole, "dates", step))
        total = add_grad(total, member, trade_gain, basis_rows[step], there, step == owners - 1)
    return total


def solution(mesh):
    return jax.shard_map(
        on_device,
        mesh=mesh,
        in_specs=(
            P("dates", "groups", None),
            P("trades", None),
            P("trades"),
            P("trades"),
            P("dates", None),
            P(),
            P(),
        ),
        out_specs=P(("groups", "trades"), "dates"),
        check_vma=False,
    )
```

```python
import functools
import math

import jax
import jax.numpy as jnp
from jax import lax
from jax.experimental import pallas as pl
from jax.experimental.pallas import tpu as pltpu
from jax.sharding import PartitionSpec as P

LAG_MAX = 2
ROWS = 1024
PIECES = 4
ORDER_IN = (0, 2, 1, 3, 6, 7, 5, 4)
ORDER_OUT = (0, 1, 2, 3, 7, 6, 4, 5)
NT = (((1,), (1,)), ((), ()))
TN = (((0,), (0,)), ((), ()))
TT = (((0,), (1,)), ((), ()))
PARAMS = pltpu.CompilerParams(vmem_limit_bytes=40 * 1024 * 1024)
SCALAR = pl.BlockSpec(memory_space=pltpu.SMEM)
LOCAL = pl.BlockSpec(memory_space=pltpu.VMEM)


def in_hbm(*arrays):
    return [pltpu.with_memory_space_constraint(array, pltpu.HBM) for array in arrays]


def kept(array):
    return pltpu.VMEM(array.shape, array.dtype)


def offsets_of(order, peers):
    base = order if peers % len(order) == 0 else range(peers)
    return [first + offset for first in range(0, peers, len(base)) for offset in base]


def rounds_of(offsets, owners):
    assert len(offsets) % owners == 0
    return [tuple(offsets[at : at + owners]) for at in range(0, len(offsets), owners)]


def shared_of(peers, owners):
    return range(1, 1 + (peers - 1) % owners)


def target_of(index, offset, peers):
    return index ^ offset if peers & (peers - 1) == 0 else lax.rem(index + offset, peers)


def source_of(index, offset, peers):
    return index ^ offset if peers & (peers - 1) == 0 else lax.rem(index + (peers - offset), peers)


def offset_at(core, offsets):
    found = jnp.int32(offsets[0])
    for other, offset in enumerate(offsets):
        found = jnp.where(core == other, jnp.int32(offset), found)
    return found


def exchanged(array, offsets, peers):
    owners = len(offsets)
    pairs = [
        (trade * owners + core, int(target_of(trade, offsets[core], peers)) * owners + core)
        for trade in range(peers)
        for core in range(owners)
    ]
    return lax.ppermute(array, ("trades", "dates"), pairs)


def together_kernel(count, *refs):
    for at in range(count):
        refs[-1][at] = refs[at - 1 - count][...]


def together_of(arrays, others):
    shape = (len(arrays),) + arrays[0].shape
    return pl.pallas_call(
        functools.partial(together_kernel, len(arrays)),
        in_specs=[LOCAL] * (len(arrays) + len(others)),
        out_specs=LOCAL,
        out_shape=pltpu.VMEM(shape, arrays[0].dtype),
        compiler_params=PARAMS,
    )(*others, *arrays)


def shifted(array, axis, step):
    peers = lax.axis_size(axis)
    return lax.ppermute(array, axis, [(i, (i + step) % peers) for i in range(peers)])


def gain_of_trades(gain, types):
    rows = jnp.zeros((gain.shape[0], types.shape[1]), jnp.float32)
    for which in range(gain.shape[1]):
        rows = jnp.where(types == which, gain[:, which : which + 1], rows)
    return rows


def load_kernel(*refs):
    given, (member_ref, gain_rows_ref, *copies), (set_ref, arrived) = refs[:7], refs[7:-2], refs[-2:]
    set_count, trades = member_ref.shape
    type_ref, gain_ref = copies[2:4]
    moves = [
        pltpu.make_async_copy(source, target, arrived.at[at])
        for at, (source, target) in enumerate(zip(given, copies + [set_ref], strict=True))
    ]
    basis_move, coef_move, type_move, gain_move, lags_move, limits_move, set_move = moves
    for move in (set_move, type_move, gain_move, basis_move, coef_move, lags_move, limits_move):
        move.start()
    set_move.wait()
    member = lax.broadcasted_iota(jnp.int32, (set_count, trades), 0) == set_ref[...]
    member_ref[...] = member.astype(jnp.float32).astype(jnp.bfloat16)
    type_move.wait()
    gain_move.wait()
    gain_rows_ref[...] = gain_of_trades(gain_ref[...], type_ref[...])
    basis_move.wait()
    coef_move.wait()
    lags_move.wait()
    limits_move.wait()


def load(basis, coef, sets, types, gain, lags, limits):
    trades = coef.shape[0]
    return pl.pallas_call(
        load_kernel,
        in_specs=[pl.BlockSpec(memory_space=pl.ANY)] * 7,
        out_specs=[LOCAL] * 8,
        out_shape=[
            pltpu.VMEM((limits.shape[1], trades), jnp.bfloat16),
            pltpu.VMEM((gain.shape[0], trades), jnp.float32),
        ]
        + [kept(array) for array in (basis, coef, types, gain, lags, limits)],
        scratch_shapes=[pltpu.VMEM(sets.shape, sets.dtype), pltpu.SemaphoreType.DMA((7,))],
        compiler_params=PARAMS,
        cost_estimate=pl.CostEstimate(flops=coef.size * 512, bytes_accessed=coef.size * 2, transcendentals=0),
    )(*in_hbm(basis, coef, types, gain, lags, limits, sets))


def net_kernel(rounds, peers, me_ref, trade_ref, coef_ref, type_ref, member_ref, lags_ref, gain_rows_ref, *refs):
    owners = len(rounds[0])
    bases, gains, outs = refs[:owners], refs[owners : 2 * owners - 1], refs[2 * owners - 1 :]
    me, trade = me_ref[0], trade_ref[0]
    coef, member, lags = coef_ref[...], member_ref[...], lags_ref[...]
    local_dates, paths, depth = bases[0].shape
    dates = owners * local_dates
    block_paths = paths // peers
    trades, set_count = coef.shape[0], member.shape[0]
    gain = [gain_rows_ref[...]] + [gain_of_trades(ref[...], type_ref[...]) for ref in gains]
    gain = jnp.concatenate(gain, axis=0)
    masks = [(lags == value).astype(jnp.float32) for value in range(1, LAG_MAX + 1)]
    holder = [lax.rem(me + (owners - place), owners) for place in range(owners)]
    earlier = [(owner > 0).astype(jnp.float32) for owner in holder]
    together = max(1, ROWS // (dates * block_paths))
    for first in range(0, len(rounds), together):
        chunk = rounds[first : first + together]
        rows = []
        for offsets in chunk:
            target = target_of(trade, offset_at(me, offsets), peers)
            at = pl.ds(pl.multiple_of(target * block_paths, block_paths), block_paths)
            rows += [ref[:, at, :].reshape(local_dates * block_paths, depth) for ref in bases]
        rows = jnp.concatenate(rows, axis=0)
        raw = lax.dot_general(rows, coef, NT, preferred_element_type=jnp.float32)
        prices = raw.reshape(len(chunk), dates, block_paths, trades) * gain[None, :, None, :]
        prices = prices.astype(jnp.bfloat16).reshape(rows.shape[0], trades)
        netted = lax.dot_general(prices, member, NT, preferred_element_type=jnp.float32)
        netted = netted.reshape(len(chunk), dates, block_paths, set_count)
        for at, out_ref in enumerate(outs[first : first + together]):
            for date in range(dates):
                place, local = divmod(date, local_dates)
                value = netted[at, date]
                for lag, mask in enumerate(masks, 1):
                    if local >= lag:
                        value = value - mask * netted[at, date - lag]
                    else:
                        before = ((place + 1) % owners + 1) * local_dates + local - lag
                        value = value - (mask * earlier[place]) * netted[at, before]
                row = (holder[place] * local_dates + local) * block_paths
                out_ref[pl.ds(pl.multiple_of(row, block_paths), block_paths)] = value


def net(rounds, peers, me, trade, coef, types, member, lags, gain_rows, bases, later_gains):
    owners = len(bases)
    local_dates, paths, _ = bases[0].shape
    rows = owners * local_dates * paths // peers
    return pl.pallas_call(
        functools.partial(net_kernel, rounds, peers),
        in_specs=[SCALAR] * 2 + [LOCAL] * (4 + 2 * owners),
        out_specs=[LOCAL] * len(rounds),
        out_shape=[pltpu.VMEM((rows, member.shape[0]), jnp.float32)] * len(rounds),
        compiler_params=PARAMS,
    )(me, trade, coef, types, member, lags, gain_rows, *bases, *later_gains)


def adjoint_kernel(scale, block_paths, lags_ref, limits_ref, *refs):
    excess = refs[0][...]
    for ref in refs[1:-1]:
        excess = excess + ref[...]
    rows = excess.shape[0]
    masks = [(lags_ref[...] == value).astype(jnp.float32) for value in range(1, LAG_MAX + 1)]
    direct = jnp.maximum(2.0 * excess - limits_ref[...], 0.0) * scale
    direct = [direct[first : first + block_paths] for first in range(0, rows, block_paths)]
    adjoints = []
    for date, adjoint in enumerate(direct):
        for value, mask in enumerate(masks, 1):
            if date + value < len(direct):
                adjoint = adjoint - mask * direct[date + value]
        adjoints.append(adjoint)
    refs[-1][...] = jnp.concatenate(adjoints, axis=0).astype(jnp.bfloat16)


def adjoint_of(sums, lags, limits, scale, block_paths):
    return pl.pallas_call(
        functools.partial(adjoint_kernel, scale, block_paths),
        in_specs=[LOCAL] * (2 + len(sums)),
        out_specs=LOCAL,
        out_shape=pltpu.VMEM(sums[0].shape, jnp.bfloat16),
        compiler_params=PARAMS,
    )(lags, limits, *sums)


def ready_kernel(rounds, near, peers, me_ref, trade_ref, type_ref, *refs):
    owners = len(rounds[0])
    gain_refs, basis_refs = refs[:owners], refs[owners : 2 * owners]
    gain_ref, *out_refs = refs[2 * owners :]
    local_dates, paths, _ = basis_refs[0].shape
    own_depth = out_refs[0].shape[1]
    block_paths = paths // peers
    local_rows = local_dates * block_paths
    dates = owners * local_dates
    me, trade = me_ref[0], trade_ref[0]
    columns = pl.ds(pl.multiple_of(me * own_depth, own_depth), own_depth)
    for step, out_ref in enumerate(out_refs):
        core = lax.rem(me + (owners - step), owners)
        for at, offsets in enumerate(rounds if step else near + rounds):
            source = source_of(trade, offset_at(core, offsets), peers)
            span = pl.ds(pl.multiple_of(source * block_paths, block_paths), block_paths)
            for place, ref in enumerate(basis_refs):
                row = at * owners * local_rows + lax.rem(me + (owners - place), owners) * local_rows
                block = ref[:, span, columns].reshape(local_rows, own_depth)
                out_ref[pl.ds(pl.multiple_of(row, local_rows), local_rows)] = block
    rest = jnp.concatenate([gain_of_trades(ref[...], type_ref[...]) for ref in gain_refs], axis=0)
    pieces = []
    for _ in range(3):
        piece = rest.astype(jnp.bfloat16).astype(jnp.float32)
        pieces.append(piece)
        rest = rest - piece
    pieces = jnp.concatenate(pieces, axis=0).astype(jnp.bfloat16)
    shape = (3 * dates, gain_ref.shape[1])
    want = lax.rem(lax.div(lax.broadcasted_iota(jnp.int32, shape, 1), block_paths), dates)
    have = lax.rem(lax.broadcasted_iota(jnp.int32, shape, 0), dates)
    place, local = lax.div(have, local_dates), lax.rem(have, local_dates)
    have = lax.rem(me + owners - place, owners) * local_dates + local
    expand = (want == have).astype(jnp.float32).astype(jnp.bfloat16)
    gain_ref[...] = lax.dot_general(pieces, expand, TN, preferred_element_type=jnp.float32)


def ready(rounds, near, peers, me, trade, types, gains, bases):
    owners = len(bases)
    local_dates, paths, depth = bases[0].shape
    block_rows = owners * local_dates * paths // peers
    counts = [len(rounds) + len(near)] + [len(rounds)] * (owners - 1)
    return pl.pallas_call(
        functools.partial(ready_kernel, rounds, near, peers),
        in_specs=[SCALAR] * 2 + [LOCAL] * (1 + 2 * owners),
        out_specs=[LOCAL] * (1 + owners),
        out_shape=[pltpu.VMEM((types.shape[1], math.lcm(block_rows, 128)), jnp.float32)]
        + [pltpu.VMEM((block_rows * count, depth // owners), jnp.bfloat16) for count in counts],
        compiler_params=PARAMS,
        cost_estimate=pl.CostEstimate(flops=types.shape[1] * 256 * 1024, bytes_accessed=0, transcendentals=0),
    )(me, trade, types, *gains, *bases)


def grad_kernel(carry, last, member_ref, gain_ref, basis_ref, *refs):
    out_ref, *scratch = refs[-3:] if last else refs[-1:]
    adjoint_refs = refs[carry : -3 if last else -1]
    rows, set_count = adjoint_refs[0].shape
    trades = member_ref.shape[1]
    gain = gain_ref[...]
    period = gain.shape[1]
    member = member_ref[...]
    total = refs[0][...] if carry else None
    together = max(1, ROWS // rows)
    for at in range(0, len(adjoint_refs), together):
        adjoint = jnp.concatenate([ref[...] for ref in adjoint_refs[at : at + together]], axis=0)
        count = adjoint.shape[0]
        spread = lax.dot_general(member, adjoint, TT, preferred_element_type=jnp.float32)
        scaled = [
            (spread[:, left : left + period] * gain).astype(jnp.bfloat16) for left in range(0, count, period)
        ]
        scaled = jnp.concatenate(scaled, axis=1)
        basis = basis_ref[pl.ds(at * rows, count)]
        if last and at + together >= len(adjoint_refs):
            sum_ref, written = scratch
            size = trades // written.shape[0]
            moves = []
            for piece in range(written.shape[0]):
                span = pl.ds(piece * size, size)
                left, right = piece * size, (piece + 1) * size
                part = jnp.dot(scaled[left:right], basis, preferred_element_type=jnp.float32)
                sum_ref[span] = part if total is None else total[left:right] + part
                moves.append(pltpu.make_async_copy(sum_ref.at[span], out_ref.at[span], written.at[piece]))
                moves[-1].start()
            for move in moves:
                move.wait()
            return
        part = jnp.dot(scaled, basis, preferred_element_type=jnp.float32)
        total = part if total is None else total + part
    out_ref[...] = total


def add_grad(total, member, gain, basis, adjoints, last):
    carry = int(total is not None)
    trades, own_depth = member.shape[1], basis.shape[1]
    shape = (trades, own_depth)
    count = len(adjoints) * adjoints[0].shape[0]
    pieces = math.gcd(trades // 128, PIECES) if trades % 128 == 0 else 1
    return pl.pallas_call(
        functools.partial(grad_kernel, carry, last),
        in_specs=[LOCAL] * (3 + carry + len(adjoints)),
        out_specs=pl.BlockSpec(memory_space=pl.ANY) if last else LOCAL,
        out_shape=jax.ShapeDtypeStruct(shape, jnp.float32) if last else pltpu.VMEM(shape, jnp.float32),
        scratch_shapes=[pltpu.VMEM(shape, jnp.float32), pltpu.SemaphoreType.DMA((pieces,))] if last else [],
        compiler_params=PARAMS,
        cost_estimate=pl.CostEstimate(
            flops=2 * trades * count * (member.shape[0] + own_depth),
            bytes_accessed=4 * trades * own_depth,
            transcendentals=0,
        ),
    )(member, gain, basis, *([total] if carry else []), *adjoints)


def on_device(basis_values, coefficients, set_map, trade_type, type_gain, set_lags, thresholds):
    local_dates, path_count, _ = basis_values.shape
    trades = coefficients.shape[0]
    set_count = thresholds.shape[0]
    peers = lax.axis_size("trades")
    owners = lax.axis_size("dates")
    rounds_in = rounds_of(offsets_of(ORDER_IN, peers), owners)
    shared = shared_of(peers, owners)
    rounds_out = [offset for offset in offsets_of(ORDER_OUT, peers) if offset > len(shared)]
    rounds_out = rounds_of(rounds_out, owners)
    near = [(offset,) * owners for offset in shared]
    block_paths = path_count // peers
    scale = 2.0 / math.sqrt(local_dates * owners * path_count)
    me = lax.axis_index("dates").astype(jnp.int32).reshape(1)
    trade = lax.axis_index("trades").astype(jnp.int32).reshape(1)

    bases = [shifted(basis_values, "dates", step) for step in range(1, owners)]
    gains = [shifted(type_gain, "dates", step) for step in range(1, owners)]
    member, gain_rows, basis, coef, types, gain, lags, limits = load(
        basis_values,
        coefficients,
        set_map.reshape(1, trades),
        trade_type.reshape(1, trades),
        type_gain,
        set_lags.reshape(1, set_count),
        thresholds.reshape(1, set_count),
    )
    bases, gains = [basis] + bases, [gain] + gains
    partials = net(rounds_in, peers, me, trade, coef, types, member, lags, gain_rows, bases, gains[1:])
    arrived = [
        exchanged((partial * 0.5).astype(jnp.float16), offsets, peers)
        for partial, offsets in zip(partials, rounds_in, strict=True)
    ]
    trade_gain, *basis_rows = ready(rounds_out, near + [(0,) * owners], peers, me, trade, types, gains, bases)
    excess = functools.reduce(jnp.add, [part.astype(jnp.float32) for part in arrived])
    excess, trade_gain, *basis_rows = lax.optimization_barrier((excess, trade_gain, *basis_rows))
    sums = [excess] + [shifted(excess, "dates", step) for step in range(1, owners)]
    adjoint = adjoint_of(sums, lags, limits, scale, block_paths)
    close = [exchanged(adjoint, offsets, peers) for offsets in near] + [adjoint]
    apart = [exchanged(adjoint, offsets, peers) for offsets in rounds_out]
    whole = together_of(apart, close)
    total = add_grad(None, member, trade_gain, basis_rows[0], close + apart, False)
    for step in range(1, owners):
        there = list(shifted(whole, "dates", step))
        total = add_grad(total, member, trade_gain, basis_rows[step], there, step == owners - 1)
    return total


def solution(mesh):
    return jax.shard_map(
        on_device,
        mesh=mesh,
        in_specs=(
            P("dates", "groups", None),
            P("trades", None),
            P("trades"),
            P("trades"),
            P("dates", None),
            P(),
            P(),
        ),
        out_specs=P(("groups", "trades"), "dates"),
        check_vma=False,
    )
```
